128 devices in a mesh: band: 4 (over x), lon: 32 (over y, z, core).
Axes of the slice: x: 4, y: 4, z: 4, core: 2. Of those that a mesh axis runs over, the one named last changes fastest.
Arguments:
- members: bfloat16 [6144, 48, 256], P(('band', 'lon')), may hold values from -6 to 6
- obs_perts: bfloat16 [6144, 32, 256], P(('band', 'lon')), may hold values from -6 to 6
- innovations: bfloat16 [6144, 32], P(('band', 'lon')), may hold values from -12 to 12
- lists: int32 [1024, 64], P(('band', 'lon')), may hold values from 0 to 6143, as said below
- placement: int32 [6144], replicated, may hold values from 0 to 6143, as said below
- obs_taper: float32 [1024, 64, 32], P(('band', 'lon')), may hold values from 0.01 to 0.2
- state_taper: float32 [1024, 64], P(('band', 'lon')), may hold values from 0.2 to 1
Outputs:
- analysis: bfloat16 [6144, 48, 256], P(('band', 'lon'))
The draws below stay inside these ranges and needn't reach their ends.
Inputs may be any that keep to these rules, and one draw needn't show every extreme that they name: `lists`: number the groups of 8 consecutive regions like the devices (band index times the lon count plus lon index) and call row // 48 a row's device. A group's entries name only blocks on the devices at band offset -1, 0 or 1 and lon offset -1, 0 or 1 (lon taken cyclically) from the group's own; from each such device that exists they name exactly 16 distinct blocks; every region names all 16 blocks of its own device; the 64 entries of one region are distinct. `placement`: A permutation of the block ids.
All inputs are finite; a program needn't handle non-finite values. Where the reference program divides by a largest or mean magnitude, that divisor is 1e-20 or more.
Results may differ from the reference program's by a relative error of at most 0.0055.
Values may be sent and summed in bfloat16 or wider, within the bound.
No kernel may reach another device: no remote copies, remote signals or barrier semaphores. Data moves between devices by JAX's collectives and lax.ppermute only.
A program may use at most 128 MiB of HBM per device.

```python
import math
import jax
import jax.numpy as jnp
from jax import lax

K = 256
S = 48
P_SIZE = 32
NL = 64
R_DEV = 8
B_DEV = 48
NS_ITERS = 5
CAP = 16
NBLK = 6144
REGIONS = 1024
N_BAND = 4
N_LON = 32


def shared_order(key):
    return jax.random.permutation(jax.random.fold_in(key, 101), NBLK).astype(jnp.int32)


def draw_placement(key, part):
    ordering = shared_order(key)
    return ordering


def draw_lists(key, part):
    ordering = shared_order(key)
    key = jax.random.fold_in(key, 11)
    inverse = jnp.argsort(ordering, stable=True).astype(jnp.int32)
    group_count = REGIONS // R_DEV
    others_total = 8 * CAP
    classes = jnp.arange(9, dtype=jnp.int32)
    other_class = jnp.concatenate([classes[:4], classes[5:]])
    slot_number = jnp.arange(others_total, dtype=jnp.int32)

    def inside_draw(sub_key):
        return jax.random.permutation(sub_key, B_DEV)[:CAP].astype(jnp.int32)

    def one_group(group_index):
        group_key = jax.random.fold_in(key, group_index)
        key_rows, key_fill, key_shuffle = jax.random.split(group_key, 3)
        band_home = group_index // N_LON
        lon_home = group_index % N_LON
        band_near = band_home + classes // 3 - 1
        lon_near = (lon_home + classes % 3 - 1) % N_LON
        present = (band_near >= 0) & (band_near < N_BAND)
        holder = jnp.clip(band_near, 0, N_BAND - 1) * N_LON + lon_near
        inside_rows = jax.vmap(inside_draw)(jax.random.split(key_rows, 9))
        block_rows = holder[:, None] * B_DEV + inside_rows
        own_rows = block_rows[4]
        other_rows = block_rows[other_class].reshape(-1)
        other_present = jnp.repeat(present[other_class], CAP)
        fill_keys = jax.random.split(key_fill, R_DEV)
        shuffle_keys = jax.random.split(key_shuffle, R_DEV)

        def one_region(region, fill_key, shuffle_key):
            shuffled = jax.random.permutation(fill_key, others_total).astype(jnp.int32)
            assigned = slot_number % R_DEV == region
            priority = jnp.where(other_present & assigned, shuffled, jnp.where(other_present, others_total + shuffled, 2 * others_total + shuffled))
            chosen = jnp.argsort(priority, stable=True)[:NL - CAP]
            picked = jnp.concatenate([own_rows, other_rows[chosen]])
            return picked[jax.random.permutation(shuffle_key, NL)]
        rows_out = jax.vmap(one_region)(jnp.arange(R_DEV, dtype=jnp.int32), fill_keys, shuffle_keys)
        return jnp.take(inverse, rows_out, axis=0)
    blocks = jax.vmap(one_group)(jnp.arange(group_count, dtype=jnp.int32))
    return blocks.reshape(REGIONS, NL).astype(jnp.int32)


def shard_levels(stream_key, extent, cuts, least, largest):
    gain, own = 1.0, jax.random.fold_in(stream_key, 6)
    for position, shards_of in cuts:
        heights = jnp.exp(jax.random.uniform(jax.random.fold_in(own, position), (shards_of,), jnp.float32, least / len(cuts), largest / len(cuts)))
        gain = gain * jnp.repeat(heights, extent[position] // shards_of).reshape([-1 if axis == position else 1 for axis in range(len(extent))])
    return gain


def scatter_about(key, extent, deviation, most, shards=(), kind=jnp.bfloat16):
    array = deviation * jax.random.normal(key, extent, jnp.float32)
    if shards:
        array = array * shard_levels(key, extent, shards, -0.22, 0.18)
    return jnp.clip(array, -most, most).astype(kind)


def setup_inputs(seed: int = 0) -> dict:
    keys = jax.random.split(jax.random.key(seed), 8)
    return {
        "members": scatter_about(keys[0], (NBLK, S, K), 1.0, 6.0, ((0, 128),)),
        "obs_perts": scatter_about(keys[1], (NBLK, P_SIZE, K), 1.0, 6.0, ((0, 128),)),
        "innovations": scatter_about(keys[2], (NBLK, P_SIZE), 3.0, 12.0, ((0, 128),)),
        "lists": draw_lists(jax.random.fold_in(keys[7], 71), 0),
        "placement": draw_placement(jax.random.fold_in(keys[7], 71), 0),
        "obs_taper": jnp.clip(jnp.exp(math.log(0.2) - 2.9957323 * jax.random.uniform(keys[5], (REGIONS, NL, P_SIZE), jnp.float32) ** shard_levels(keys[5], (REGIONS, NL, P_SIZE), ((0, 128),), -0.2, 0.2)), 0.01, 0.2),
        "state_taper": jnp.clip(jnp.exp(math.log(1.0) - 1.609438 * jax.random.uniform(keys[6], (REGIONS, NL), jnp.float32) ** shard_levels(keys[6], (REGIONS, NL), ((0, 128),), -0.2, 0.2)), 0.2, 1.0),
    }


def inverse_root(matrix, identity):
    current = matrix
    estimate = identity
    for iteration in range(NS_ITERS):
        factor = 1.5 * identity - 0.5 * jnp.dot(estimate, current, precision=lax.Precision.HIGHEST)
        current = jnp.dot(current, factor, precision=lax.Precision.HIGHEST)
        estimate = jnp.dot(factor, estimate, precision=lax.Precision.HIGHEST)
    return estimate

def region_mix(obs_blocks, innov_blocks, weights):
    identity = jnp.eye(K, dtype=jnp.float32)
    obs_float = obs_blocks.astype(jnp.float32)
    gram_matrix = jnp.einsum('jpk,jpl->kl', obs_float * weights[:, :, None], obs_float, precision=lax.Precision.HIGHEST)
    projection = jnp.einsum('jp,jpk->k', weights * innov_blocks.astype(jnp.float32), obs_float, precision=lax.Precision.HIGHEST)
    system = (K - 1.0) * identity + gram_matrix
    scale_top = jnp.max(lax.optimization_barrier(jnp.sum(jnp.abs(system), axis=1)))
    inverse_sqrt = inverse_root(system / scale_top, identity) / jnp.sqrt(scale_top)
    halfway = jnp.dot(inverse_sqrt, projection, precision=lax.Precision.HIGHEST)
    mean_weights = jnp.dot(inverse_sqrt, halfway, precision=lax.Precision.HIGHEST)
    mixing = jnp.sqrt(K - 1.0) * inverse_sqrt - identity + mean_weights[:, None]
    return mixing.astype(jnp.bfloat16)

def reference(members, obs_perts, innovations, lists, placement, obs_taper, state_taper):
    group_count = REGIONS // R_DEV
    entries = R_DEV * NL
    row_ids = jnp.take(placement, lists, axis=0).astype(jnp.int32).reshape(group_count, entries)
    weights_all = obs_taper.reshape(group_count, R_DEV, NL, P_SIZE)
    tapers_all = state_taper.reshape(group_count, R_DEV, NL)

    def one_region(packed_region):
        rows_here, weights, tapers = packed_region
        mixing = region_mix(obs_perts[rows_here], innovations[rows_here], weights)
        portion = jnp.einsum('jsk,kl->jsl', members[rows_here].astype(jnp.float32), mixing.astype(jnp.float32))
        return (portion * tapers[:, None, None]).astype(jnp.bfloat16)

    def one_group(summed, packed):
        group_rows, group_weights, group_tapers = packed
        region_rows = group_rows.reshape(R_DEV, NL)
        portions = lax.map(one_region, (region_rows, group_weights, group_tapers))
        portions = lax.optimization_barrier(portions).reshape(entries, S, K)
        matching = group_rows[:, None] == group_rows[None, :]
        first_match = jnp.argmax(matching, axis=1).astype(jnp.int32)
        shares = jnp.zeros((entries, S, K), jnp.float32).at[first_match].add(portions.astype(jnp.float32))
        shares = lax.optimization_barrier(shares.astype(jnp.bfloat16))
        summed = summed.at[group_rows].add(shares.astype(jnp.float32))
        return (summed, None)
    start = jnp.zeros(members.shape, jnp.float32)
    summed, unused = lax.scan(one_group, start, (row_ids, weights_all, tapers_all))
    return (members.astype(jnp.float32) + summed).astype(jnp.bfloat16)
```

```python
import functools

import jax
import jax.numpy as jnp
from jax import lax
from jax.experimental import pallas as pl
from jax.experimental.pallas import tpu as pltpu
from jax.sharding import PartitionSpec as P

NS_ITERS = 5
CAP = 16
CLASSES = 9
BAND_SLOTS = 3 * CAP
CLASS_STRIDE = 64
KEYS = 640
META_LANES = 256

F32 = jnp.float32
BF16 = jnp.bfloat16
VMEM_SPEC = pl.BlockSpec(memory_space=pltpu.VMEM)
SMEM_SPEC = pl.BlockSpec(memory_space=pltpu.SMEM)


def dot(a, b):
    return jnp.dot(a, b, preferred_element_type=F32)


def call(kernel, outs, in_specs, name, flops, bytes_accessed, scratch=(), aliases=None):
    return pl.pallas_call(
        kernel,
        out_shape=outs,
        in_specs=in_specs,
        out_specs=jax.tree.map(lambda _: VMEM_SPEC, outs),
        scratch_shapes=list(scratch),
        input_output_aliases=aliases or {},
        compiler_params=pltpu.CompilerParams(vmem_limit_bytes=40 * 1024 * 1024),
        cost_estimate=pl.CostEstimate(
            flops=flops, bytes_accessed=bytes_accessed, transcendentals=0
        ),
        name=name,
    )


def table_kernel(regions, list_len, key_col, key_row, taper, state, weights, meta):
    entries = regions * list_len
    key_down = lax.broadcasted_iota(jnp.int32, (KEYS, entries), 0)
    hot_t = jnp.where(key_down == key_row[...], 1.0, 0.0).astype(BF16)
    counts = dot(hot_t, jnp.ones((entries, 128), BF16))
    present = jnp.minimum(counts, 1.0)
    row = lax.broadcasted_iota(jnp.int32, (KEYS, KEYS), 0)
    col = lax.broadcasted_iota(jnp.int32, (KEYS, KEYS), 1)
    before = (col < row) & (col // CLASS_STRIDE == row // CLASS_STRIDE)
    rank = dot(jnp.where(before, 1.0, 0.0).astype(BF16), present.astype(BF16))
    key_id = lax.broadcasted_iota(jnp.int32, (KEYS, 128), 0)
    slot = rank + (CAP * (key_id // CLASS_STRIDE)).astype(F32)
    inside = (key_id % CLASS_STRIDE).astype(F32)
    key_across = lax.broadcasted_iota(jnp.int32, (entries, KEYS), 1)
    hot = jnp.where(key_across == key_col[...], 1.0, 0.0).astype(BF16)
    entry_slot = dot(hot, slot.astype(BF16))
    lane = lax.broadcasted_iota(jnp.int32, (1, 128), 1).astype(F32)
    group = (lax.broadcasted_iota(jnp.int32, (1, 128), 1) // 32).astype(F32)
    meta[...] = jnp.zeros_like(meta)
    for c in range(2):
        match = (slot == lane + 128.0 * c) & (present > 0.0)
        rows = jnp.sum(jnp.where(match, inside, 0.0), axis=0, keepdims=True)
        meta[8:9, 128 * c : 128 * (c + 1)] = rows
    for r in range(regions):
        mine = entry_slot[r * list_len : (r + 1) * list_len]
        w = taper[r]
        for c in range(CLASSES * CAP // 4):
            hit = mine == group + 4.0 * c
            weights[r : r + 1, 128 * c : 128 * (c + 1)] = jnp.sum(
                jnp.where(hit, w, 0.0), axis=0, keepdims=True
            )
        t = state[r * list_len : (r + 1) * list_len]
        for c in range(2):
            hit = mine == lane + 128.0 * c
            meta[r : r + 1, 128 * c : 128 * (c + 1)] = jnp.sum(
                jnp.where(hit, t, 0.0), axis=0, keepdims=True
            )


def gather_blocks(sources, table, rows, first_slot, obs_rows, out):
    blocks = sources[0].shape[0] // (obs_rows + 1)
    down = lax.broadcasted_iota(jnp.int32, (blocks, META_LANES), 0).astype(F32)
    hot = jnp.where(down == rows, 1.0, 0.0).astype(BF16)
    for band in range(3):
        source = sources[band]

        def one(i, carry, source=source, band=band):
            slot = first_slot + CAP * band + i
            at = pl.multiple_of(table[8, slot].astype(jnp.int32) * obs_rows, obs_rows)
            to = pl.multiple_of((CAP * band + i) * obs_rows, obs_rows)
            out[pl.ds(to, obs_rows), :] = source[pl.ds(at, obs_rows), :]
            return carry

        lax.fori_loop(0, CAP, one, 0, unroll=True)
        innov = source[blocks * obs_rows :, :]
        picked = lax.dot_general(
            hot, innov, (((0,), (0,)), ((), ())), preferred_element_type=F32
        ).astype(BF16)
        base = 3 * CAP * obs_rows + CAP * band
        start = first_slot + CAP * band
        out[base : base + CAP, :] = picked[start : start + CAP]


def select_kernel(obs_rows, below, here, above, table_w, table_e, rows_w, rows_e, to_w, to_e):
    sources = (below, here, above)
    gather_blocks(sources, table_w, rows_w[8:9, :], 2 * BAND_SLOTS, obs_rows, to_w)
    gather_blocks(sources, table_e, rows_e[8:9, :], 0, obs_rows, to_e)


def add_gram(pool, first_slot, weights, obs_rows, regions, gram, proj, start):
    count = BAND_SLOTS * obs_rows
    lanes = slice(first_slot * obs_rows, first_slot * obs_rows + count)
    y = pool[:count, :]
    y_t = jnp.concatenate(
        [y[256 * c : 256 * (c + 1)].astype(F32).T.astype(BF16) for c in range(count // 256)],
        axis=1,
    )
    innov = pool[count : count + BAND_SLOTS, :].astype(F32)
    per = 256 // obs_rows
    sub = lax.broadcasted_iota(jnp.int32, (per, 256), 0)
    which = lax.broadcasted_iota(jnp.int32, (per, 256), 1) // obs_rows
    pieces = [
        jnp.sum(jnp.where(sub == which, innov[per * c : per * (c + 1)], 0.0), axis=0, keepdims=True)
        for c in range(count // 256)
    ]
    w = weights[:, lanes]
    wd = w * jnp.concatenate(pieces, axis=1)
    high = wd.astype(BF16)
    low = (wd - high.astype(F32)).astype(BF16)
    part = dot(jnp.concatenate([high, low], axis=0), y)
    part = part[:regions] + part[regions:]
    proj[...] = part if start else proj[...] + part
    w16 = w.astype(BF16)
    for r in range(regions):
        scaled = y_t * w16[r : r + 1, :]
        product = dot(scaled, y)
        rows = slice(256 * r, 256 * (r + 1))
        gram[rows, :] = product if start else gram[rows, :] + product


def own_gram_kernel(
    obs_rows, regions, below, here, above, table, rows, weights, gram, proj, pool
):
    gather_blocks((below, here, above), table, rows[8:9, :], BAND_SLOTS, obs_rows, pool)
    add_gram(pool, BAND_SLOTS, weights, obs_rows, regions, gram, proj, True)


def total(x):
    return jnp.sum(jnp.sum(x, axis=0, keepdims=True), axis=1, keepdims=True)


def roots(grams, proj_rows, eye, ensemble):
    count = len(grams)
    base = ensemble - 1.0
    each = range(count)
    absolute = [jnp.abs(grams[i] + base * eye) for i in each]
    scale = [
        jnp.max(jnp.sum(absolute[i], axis=0, keepdims=True), axis=1, keepdims=True) for i in each
    ]
    mean = [total(grams[i] * eye) / ensemble for i in each]
    f = [(mean[i] * eye - grams[i]) / scale[i] for i in each]
    c = [1.0 - (base + mean[i]) / scale[i] for i in each]
    a = [1.0 + 0.5 * c[i] for i in each]
    g = [0.5 * f[i] for i in each]
    for step in range(NS_ITERS - 1):
        fb = [f[i].astype(BF16) for i in each]
        f2 = [dot(fb[i], fb[i]) for i in each]
        f3 = [dot(f2[i].astype(BF16), fb[i]) for i in each]
        f = [
            (1.5 * c[i] + 0.75 * c[i] * c[i]) * f[i]
            + (0.75 + 0.75 * c[i]) * f2[i]
            + 0.25 * f3[i]
            for i in each
        ]
        c = [(0.75 + 0.25 * c[i]) * c[i] * c[i] for i in each]
        fg = [dot(f[i].astype(BF16), g[i].astype(BF16)) for i in each]
        g = [
            (1.0 + 0.5 * c[i]) * g[i] + (0.5 * a[i]) * f[i] + 0.5 * fg[i] for i in each
        ]
        a = [a[i] * (1.0 + 0.5 * c[i]) for i in each]
    gb = [g[i].astype(BF16) for i in each]
    first = lax.broadcasted_iota(jnp.int32, (16, ensemble), 0) < 8

    def times(i, v):
        high = v.astype(BF16).astype(F32)
        stacked = jnp.where(first, high, v - high).astype(BF16)
        q = dot(stacked, gb[i])
        return a[i] * v + q[0:1] + q[8:9]

    half = [times(i, proj_rows[i]) for i in each]
    wbar = [times(i, half[i]) / scale[i] for i in each]
    root = [a[i] * eye + g[i] for i in each]
    column = [jnp.sum(eye * wbar[i], axis=1, keepdims=True) for i in each]
    return [
        (lax.sqrt(base / scale[i]) * root[i] - eye + column[i]).astype(BF16) for i in each
    ]


def mix_kernel(obs_rows, regions, together, west, east, weights, gram_in, proj_in, mix, gram, proj):
    gram[...] = gram_in[...]
    proj[...] = proj_in[...]
    add_gram(west, 0, weights, obs_rows, regions, gram, proj, False)
    add_gram(east, 2 * BAND_SLOTS, weights, obs_rows, regions, gram, proj, False)
    n = gram.shape[1]
    down = lax.broadcasted_iota(jnp.int32, (n, n), 0)
    across = lax.broadcasted_iota(jnp.int32, (n, n), 1)
    eye = jnp.where(down == across, 1.0, 0.0)
    for first in range(0, regions, together):
        some = range(first, first + together)
        done = roots(
            [gram[n * r : n * (r + 1), :] for r in some],
            [proj[r : r + 1, :] for r in some],
            eye,
            n,
        )
        for r, m in zip(some, done):
            mix[n * r : n * (r + 1), :] = m


def add_increment(members, table, first_slot, mix, acc, left, right, state_rows, regions):
    n = members.shape[1]
    for i in range(CAP):
        at = pl.multiple_of(table[8, first_slot + i].astype(jnp.int32) * state_rows, state_rows)
        x = members[pl.ds(at, state_rows), :].astype(F32)
        for r in range(regions):
            left[state_rows * i : state_rows * (i + 1), n * r : n * (r + 1)] = (
                x * table[r, first_slot + i]
            ).astype(BF16)
    right[...] = dot(left[...], mix[...])
    for i in range(CAP):
        at = pl.multiple_of(table[8, first_slot + i].astype(jnp.int32) * state_rows, state_rows)
        acc[pl.ds(at, state_rows), :] += right[state_rows * i : state_rows * (i + 1), :]


def middle_kernel(slots, state_rows, regions, members, *refs):
    count = len(slots)
    tables, mixes = refs[:count], refs[count : 2 * count]
    acc, left, right = refs[2 * count :]
    acc[...] = members[...].astype(F32)
    for k in range(count):
        add_increment(
            members, tables[k], slots[k], mixes[k], acc, left, right, state_rows, regions
        )


def final_kernel(slots, state_rows, regions, members, acc_in, *refs):
    count = len(slots)
    tables, mixes = refs[:count], refs[count : 2 * count]
    out, acc, left, right = refs[2 * count :]
    acc[...] = acc_in[...]
    for k in range(count):
        add_increment(
            members, tables[k], slots[k], mixes[k], acc, left, right, state_rows, regions
        )
    out[...] = acc[...].astype(BF16)


def from_band(x, step):
    devices = range(lax.axis_size("band"))
    return lax.ppermute(x, "band", [(i + step, i) for i in devices if i + step in devices])


def from_lon(x, step):
    count = lax.axis_size("lon")
    return lax.ppermute(x, "lon", [((i + step) % count, i) for i in range(count)])


def local(members, obs_perts, innovations, lists, placement, obs_taper, state_taper):
    lon_count = lax.axis_size("lon")
    band_here = lax.axis_index("band")
    lon_here = lax.axis_index("lon")
    blocks, state_rows, n = members.shape
    obs_rows = obs_perts.shape[1]
    regions, list_len = lists.shape
    entries = regions * list_len
    repeat = n // obs_rows

    payload = jnp.concatenate(
        [obs_perts.reshape(blocks * obs_rows, n), jnp.tile(innovations, (1, repeat))], axis=0
    )
    below = from_band(payload, -1)
    above = from_band(payload, 1)

    row_ids = jnp.take(placement, lists.reshape(-1), axis=0)
    holder = row_ids // blocks
    band_step = holder // lon_count - band_here
    lon_step = (holder % lon_count - lon_here + 1) % lon_count - 1
    key = ((lon_step + 1) * 3 + band_step + 1) * CLASS_STRIDE + row_ids % blocks
    weights, meta = call(
        functools.partial(table_kernel, regions, list_len),
        (
            jax.ShapeDtypeStruct((regions, CLASSES * CAP * obs_rows), F32),
            jax.ShapeDtypeStruct((16, META_LANES), F32),
        ),
        [VMEM_SPEC] * 4,
        "tables",
        10**9,
        10**6,
    )(
        key[:, None],
        key[None, :],
        jnp.tile(obs_taper, (1, 1, 128 // obs_rows)),
        state_taper.reshape(entries, 1),
    )
    meta_w = from_lon(meta, -1)
    meta_e = from_lon(meta, 1)

    sent = (BAND_SLOTS * (obs_rows + 1), n)
    sent_shape = jax.ShapeDtypeStruct(sent, BF16)
    to_w, to_e = call(
        functools.partial(select_kernel, obs_rows),
        (sent_shape, sent_shape),
        [VMEM_SPEC] * 3 + [SMEM_SPEC] * 2 + [VMEM_SPEC] * 2,
        "select",
        10**8,
        4 * 10**6,
    )(below, payload, above, meta_w, meta_e, meta_w, meta_e)
    west = from_lon(to_e, -1)
    east = from_lon(to_w, 1)

    metas = jnp.concatenate([meta_w, meta, meta_e], axis=0)
    metas_below = from_band(metas, -1)
    metas_above = from_band(metas, 1)

    gram_shape = jax.ShapeDtypeStruct((regions * n, n), F32)
    proj_shape = jax.ShapeDtypeStruct((regions, n), F32)
    gram, proj = call(
        functools.partial(own_gram_kernel, obs_rows, regions),
        (gram_shape, proj_shape),
        [VMEM_SPEC] * 3 + [SMEM_SPEC] + [VMEM_SPEC] * 2,
        "own_gram",
        2 * regions * sent[0] * n * n,
        5 * 10**6,
        [pltpu.VMEM(sent, BF16)],
    )(below, payload, above, meta, meta, weights)
    mix = call(
        functools.partial(mix_kernel, obs_rows, regions, 4),
        jax.ShapeDtypeStruct((regions * n, n), BF16),
        [VMEM_SPEC] * 5,
        "mixing",
        2 * regions * (2 * sent[0] + 12 * n) * n * n,
        5 * 10**6,
        [pltpu.VMEM((regions * n, n), F32), pltpu.VMEM((regions, n), F32)],
    )(west, east, weights, gram, proj)

    mix_below = from_band(mix, -1)
    mix_above = from_band(mix, 1)
    mix_w = from_lon(mix, -1)
    mix_e = from_lon(mix, 1)
    mix_wb = from_lon(mix_below, -1)
    mix_eb = from_lon(mix_below, 1)
    mix_wa = from_lon(mix_above, -1)
    mix_ea = from_lon(mix_above, 1)

    stacked = {-1: metas_below, 0: metas, 1: metas_above}

    def table(lon, band):
        return stacked[band][16 * (lon + 1) : 16 * (lon + 2)]

    def slots(lon, band):
        return CAP * (CLASSES - 1 - ((lon + 1) * 3 + band + 1))

    flat = members.reshape(blocks * state_rows, n)
    scratch = [
        pltpu.VMEM((CAP * state_rows, regions * n), BF16),
        pltpu.VMEM((CAP * state_rows, n), F32),
    ]
    inner = [(0, 0), (0, -1), (0, 1), (-1, 0), (1, 0)]
    group_flops = 2 * CAP * state_rows * regions * n * n
    acc = call(
        functools.partial(middle_kernel, [slots(*o) for o in inner], state_rows, regions),
        jax.ShapeDtypeStruct((blocks * state_rows, n), F32),
        [VMEM_SPEC] + [SMEM_SPEC] * 5 + [VMEM_SPEC] * 5,
        "increments",
        5 * group_flops,
        9 * 10**6,
        scratch,
    )(flat, *[table(*o) for o in inner], mix, mix_below, mix_above, mix_w, mix_e)
    outer = [(-1, -1), (1, -1), (-1, 1), (1, 1)]
    out = call(
        functools.partial(final_kernel, [slots(*o) for o in outer], state_rows, regions),
        jax.ShapeDtypeStruct((blocks * state_rows, n), BF16),
        [VMEM_SPEC] * 2 + [SMEM_SPEC] * 4 + [VMEM_SPEC] * 4,
        "finish",
        4 * group_flops,
        9 * 10**6,
        [pltpu.VMEM((blocks * state_rows, n), F32)] + scratch,
    )(flat, acc, *[table(*o) for o in outer], mix_wb, mix_eb, mix_wa, mix_ea)
    return out.reshape(members.shape)


def solution(mesh):
    in_specs = (
        P(("band", "lon"), None, None),
        P(("band", "lon"), None, None),
        P(("band", "lon"), None),
        P(("band", "lon"), None),
        P(),
        P(("band", "lon"), None, None),
        P(("band", "lon"), None),
    )
    out_specs = P(("band", "lon"), None, None)
    return jax.shard_map(local, mesh=mesh, in_specs=in_specs, out_specs=out_specs, check_vma=False)
```

```python
import functools

import jax
import jax.numpy as jnp
from jax import lax
from jax.experimental import pallas as pl
from jax.experimental.pallas import tpu as pltpu
from jax.sharding import PartitionSpec as P

NS_ITERS = 5
CAP = 16
CLASSES = 9
BAND_SLOTS = 3 * CAP
CLASS_STRIDE = 64
KEYS = 640
META_LANES = 256

F32 = jnp.float32
BF16 = jnp.bfloat16
VMEM_SPEC = pl.BlockSpec(memory_space=pltpu.VMEM)
SMEM_SPEC = pl.BlockSpec(memory_space=pltpu.SMEM)


def dot(a, b):
    return jnp.dot(a, b, preferred_element_type=F32)


def call(kernel, outs, in_specs, name, flops, bytes_accessed, scratch=(), aliases=None):
    return pl.pallas_call(
        kernel,
        out_shape=outs,
        in_specs=in_specs,
        out_specs=jax.tree.map(lambda _: VMEM_SPEC, outs),
        scratch_shapes=list(scratch),
        input_output_aliases=aliases or {},
        compiler_params=pltpu.CompilerParams(vmem_limit_bytes=40 * 1024 * 1024),
        cost_estimate=pl.CostEstimate(
            flops=flops, bytes_accessed=bytes_accessed, transcendentals=0
        ),
        name=name,
    )


def table_kernel(shape, lists, placement, state, innov, obs, meta, entry_slot, obs_copy):
    lon_count, blocks = shape
    regions, list_len = lists.shape
    entries = regions * list_len
    obs_rows = innov.shape[1]
    obs_copy[...] = obs[...]
    p = lax.broadcasted_iota(jnp.int32, (obs_rows, META_LANES), 0)
    q = lax.broadcasted_iota(jnp.int32, (obs_rows, META_LANES), 1) % obs_rows
    meta[16:, :] = dot(innov[...], jnp.where(p == q, 1.0, 0.0).astype(BF16))

    def columns(x):
        t = x.T
        return jnp.concatenate(
            [jnp.broadcast_to(t[:, r : r + 1], (list_len, 128)) for r in range(regions)], axis=0
        )

    lane = lax.broadcasted_iota(jnp.int32, (1, 128), 1).astype(F32)
    ones = jnp.ones((128, 128), BF16)
    ids = columns(lists[...].astype(F32))
    line = jnp.floor(ids * (1.0 / 128.0))
    table_rows = placement.shape[0]
    line_hot = jnp.where(line == lane, 1.0, 0.0).astype(BF16)[:, :table_rows]
    at = lane == ids - 128.0 * line
    places = placement[...].astype(F32)
    high = jnp.floor(places * (1.0 / 64.0))

    def look(part):
        found = dot(line_hot, part.astype(BF16))
        return dot(jnp.where(at, found, 0.0).astype(BF16), ones)

    row = 64.0 * look(high) + look(places - 64.0 * high)
    holder = jnp.floor((row + 0.5) * (1.0 / blocks))
    inside = row - blocks * holder
    holder_band = jnp.floor((holder + 0.5) * (1.0 / lon_count))
    band_step = holder_band - lax.axis_index("band").astype(F32)
    lon_step = holder - lon_count * holder_band - lax.axis_index("lon").astype(F32) + 1.0
    lon_step = jnp.where(lon_step < 0.0, lon_step + lon_count, lon_step)
    lon_step = jnp.where(lon_step >= lon_count, lon_step - lon_count, lon_step)
    key = (lon_step * 3.0 + band_step + 1.0) * CLASS_STRIDE + inside

    hot = jnp.concatenate(
        [jnp.where(key == lane + 128.0 * c, 1.0, 0.0) for c in range(KEYS // 128)], axis=1
    ).astype(BF16)
    counts = lax.dot_general(
        hot,
        jnp.ones((entries, 128), BF16),
        (((0,), (0,)), ((), ())),
        preferred_element_type=F32,
    )
    present = jnp.minimum(counts, 1.0)
    down = lax.broadcasted_iota(jnp.int32, (KEYS, KEYS), 0)
    across = lax.broadcasted_iota(jnp.int32, (KEYS, KEYS), 1)
    before = (across < down) & (across // CLASS_STRIDE == down // CLASS_STRIDE)
    rank = dot(jnp.where(before, 1.0, 0.0).astype(BF16), present.astype(BF16))
    key_id = lax.broadcasted_iota(jnp.int32, (KEYS, 128), 0)
    slot = rank + (CAP * (key_id // CLASS_STRIDE)).astype(F32)
    block = (key_id % CLASS_STRIDE).astype(F32)
    slots = dot(hot, slot.astype(BF16))
    entry_slot[...] = slots
    meta[0:16, :] = jnp.zeros((16, META_LANES), F32)
    tapers = columns(state[...])
    for c in range(2):
        match = (slot == lane + 128.0 * c) & (present > 0.0)
        rows = jnp.sum(jnp.where(match, block, 0.0), axis=0, keepdims=True)
        meta[8:9, 128 * c : 128 * (c + 1)] = rows
        hit = jnp.where(slots == lane + 128.0 * c, tapers, 0.0)
        for r in range(regions):
            meta[r : r + 1, 128 * c : 128 * (c + 1)] = jnp.sum(
                hit[r * list_len : (r + 1) * list_len], axis=0, keepdims=True
            )


def weight_kernel(regions, list_len, entry_slot, taper, weights):
    obs_rows = taper.shape[1]
    group = (lax.broadcasted_iota(jnp.int32, (1, 128), 1) // obs_rows).astype(F32)
    p = lax.broadcasted_iota(jnp.int32, (obs_rows, 128), 0)
    q = lax.broadcasted_iota(jnp.int32, (obs_rows, 128), 1) % obs_rows
    spread = jnp.where(p == q, 1.0, 0.0).astype(BF16)

    def across(x):
        return lax.dot_general(
            x, spread, (((0,), (0,)), ((), ())), preferred_element_type=F32
        )

    for r in range(regions):
        mine = entry_slot[r * list_len : (r + 1) * list_len, :]
        high = taper[r].astype(BF16)
        low = (taper[r] - high.astype(F32)).astype(BF16)
        w = across(high) + across(low)
        for c in range(CLASSES * CAP // 4):
            hit = mine == group + 4.0 * c
            weights[r : r + 1, 128 * c : 128 * (c + 1)] = jnp.sum(
                jnp.where(hit, w, 0.0), axis=0, keepdims=True
            )


def gather_blocks(sources, table, first_slot, obs_rows, out):
    for band in range(3):
        for i in range(CAP):
            slot = first_slot + CAP * band + i
            at = pl.multiple_of(table[8, slot].astype(jnp.int32) * obs_rows, obs_rows)
            to = (CAP * band + i) * obs_rows
            out[to : to + obs_rows, :] = sources[band][pl.ds(at, obs_rows), :]


def select_kernel(obs_rows, below, here, above, table_w, table_e, to_w, to_e):
    sources = (below, here, above)
    gather_blocks(sources, table_w, 2 * BAND_SLOTS, obs_rows, to_w)
    gather_blocks(sources, table_e, 0, obs_rows, to_e)


def transposed(y):
    return jnp.concatenate(
        [y[256 * c : 256 * (c + 1)].astype(F32).T.astype(BF16) for c in range(y.shape[0] // 256)],
        axis=1,
    )


def own_gram_kernel(obs_rows, regions, below, here, above, table, weights, gram, pool):
    gather_blocks((below, here, above), table, BAND_SLOTS, obs_rows, pool)
    y = pool[...]
    y_t = transposed(y)
    first = BAND_SLOTS * obs_rows
    w16 = weights[:, first : 2 * first].astype(BF16)
    for r in range(regions):
        gram[256 * r : 256 * (r + 1), :] = dot(y_t * w16[r : r + 1, :], y)


def innov_kernel(obs_rows, regions, meta, below, here, above, weights, pool, scaled, proj):
    blocks = here.shape[0] // 3 - 16
    down = lax.broadcasted_iota(jnp.int32, (blocks, META_LANES), 0).astype(F32)
    hot = jnp.where(down == meta[8:9, :], 1.0, 0.0).T.astype(BF16)
    per = META_LANES // obs_rows
    sub = lax.broadcasted_iota(jnp.int32, (per, META_LANES), 0)
    which = lax.broadcasted_iota(jnp.int32, (per, META_LANES), 1) // obs_rows
    pieces = []
    for n in range(CLASSES):
        source = (below, here, above)[n % 3]
        base = (16 + blocks) * (n // 3) + 16
        innov = source[base : base + blocks, :].astype(BF16)
        picked = dot(hot[CAP * n : CAP * (n + 1)], innov)
        for c in range(CAP // per):
            part = jnp.where(sub == which, picked[per * c : per * (c + 1)], 0.0)
            pieces.append(jnp.sum(part, axis=0, keepdims=True))
    wd = weights[...] * jnp.concatenate(pieces, axis=1)
    high = wd.astype(BF16)
    both = jnp.concatenate([high.astype(F32), wd - high.astype(F32)], axis=0).astype(BF16)
    scaled[...] = both
    first = BAND_SLOTS * obs_rows
    part = dot(both[:, first : 2 * first], pool[...])
    proj[...] = part[:regions] + part[regions:]


def total(x):
    return jnp.sum(jnp.sum(x, axis=0, keepdims=True), axis=1, keepdims=True)


def roots(grams, proj_rows, eye, ensemble):
    count = len(grams)
    base = ensemble - 1.0
    each = range(count)
    absolute = [jnp.abs(grams[i] + base * eye) for i in each]
    scale = [
        jnp.max(jnp.sum(absolute[i], axis=0, keepdims=True), axis=1, keepdims=True) for i in each
    ]
    mean = [total(grams[i] * eye) / ensemble for i in each]
    f = [(mean[i] * eye - grams[i]) / scale[i] for i in each]
    c = [1.0 - (base + mean[i]) / scale[i] for i in each]
    a = [1.0 + 0.5 * c[i] for i in each]
    g = [0.5 * f[i] for i in each]
    for step in range(NS_ITERS - 1):
        fb = [f[i].astype(BF16) for i in each]
        f2 = [dot(fb[i], fb[i]) for i in each]
        f3 = [dot(f2[i].astype(BF16), fb[i]) for i in each]
        f = [
            (1.5 * c[i] + 0.75 * c[i] * c[i]) * f[i]
            + (0.75 + 0.75 * c[i]) * f2[i]
            + 0.25 * f3[i]
            for i in each
        ]
        c = [(0.75 + 0.25 * c[i]) * c[i] * c[i] for i in each]
        fg = [dot(f[i].astype(BF16), g[i].astype(BF16)) for i in each]
        g = [
            (1.0 + 0.5 * c[i]) * g[i] + (0.5 * a[i]) * f[i] + 0.5 * fg[i] for i in each
        ]
        a = [a[i] * (1.0 + 0.5 * c[i]) for i in each]
    gb = [g[i].astype(BF16) for i in each]
    first = lax.broadcasted_iota(jnp.int32, (16, ensemble), 0) < 8

    def times(i, v):
        high = v.astype(BF16).astype(F32)
        stacked = jnp.where(first, high, v - high).astype(BF16)
        q = dot(stacked, gb[i])
        return a[i] * v + q[0:1] + q[8:9]

    half = [times(i, proj_rows[i]) for i in each]
    wbar = [times(i, half[i]) / scale[i] for i in each]
    return [
        lax.sqrt(base / scale[i]) * (a[i] * eye + g[i]) - eye for i in each
    ], wbar


def pack(symmetric, wbar, corner_eye, upper):
    quarter = symmetric[128:, 128:]
    merged = jnp.where(upper, symmetric[:128, :128], quarter)
    diagonal = jnp.sum(quarter * corner_eye, axis=0, keepdims=True)
    high = wbar.astype(BF16).astype(F32)
    low = wbar - high
    rows = [diagonal, high[:, :128], high[:, 128:], low[:, :128], low[:, 128:]]
    down = lax.broadcasted_iota(jnp.int32, (16, 128), 0)
    extra = jnp.zeros((16, 128), F32)
    for k, r in enumerate(rows):
        extra = jnp.where(down == k, r, extra)
    return symmetric[:128, 128:].astype(BF16), merged.astype(BF16), extra.astype(BF16)


def mix_regions(first, count, gram, proj, packed):
    n = 256
    extras = n * proj.shape[0]
    down = lax.broadcasted_iota(jnp.int32, (n, n), 0)
    across = lax.broadcasted_iota(jnp.int32, (n, n), 1)
    eye = jnp.where(down == across, 1.0, 0.0)
    upper = (down <= across)[:128, :128]
    some = range(first, first + count)
    matrices, weights = roots(
        [gram[r - first] for r in some], [proj[r : r + 1, :] for r in some], eye, n
    )
    for k, r in enumerate(some):
        right, merged, extra = pack(matrices[k], weights[k], eye[:128, :128], upper)
        packed[n * r : n * r + 128, :] = right
        packed[n * r + 128 : n * (r + 1), :] = merged
        packed[extras + 16 * r : extras + 16 * (r + 1), :] = extra


def grams_of(first, count, gram_own, weights, parts):
    out = []
    for r in range(first, first + count):
        total_r = gram_own[256 * r : 256 * (r + 1), :]
        for y, y_t, lane in parts:
            w16 = weights[r : r + 1, lane : lane + y.shape[0]].astype(BF16)
            total_r = total_r + dot(y_t * w16, y)
        out.append(total_r)
    return out


def mix_kernel(together, west, east, weights, gram_own, scaled, proj_own, packed, proj):
    regions = proj.shape[0]
    size = west.shape[0]
    part = dot(scaled[:, :size], west[...]) + dot(scaled[:, 2 * size :], east[...])
    proj[...] = proj_own[...] + part[:regions] + part[regions:]
    parts = [
        (west[...], transposed(west[...]), 0),
        (east[...], transposed(east[...]), 2 * size),
    ]
    for first in range(0, regions, together):
        grams = grams_of(first, together, gram_own, weights, parts)
        mix_regions(first, together, grams, proj, packed)


def unpack(count, packed, full):
    n = 256
    down = lax.broadcasted_iota(jnp.int32, (128, 128), 0)
    across = lax.broadcasted_iota(jnp.int32, (128, 128), 1)
    upper = down <= across
    lower = down > across
    extra = packed[n * count : (n + 16) * count, :].astype(F32)
    missing = 128 - 16 * count
    if missing:
        padded = jnp.concatenate([extra, jnp.zeros((missing, 128), F32)], axis=0)
    else:
        padded = extra
    columns = padded.T
    for k in range(count):
        right = packed[n * k : n * k + 128, :].astype(F32)
        merged = packed[n * k + 128 : n * (k + 1), :].astype(F32)
        turned = merged.T
        top = columns[:, 16 * k + 1 : 16 * k + 2] + columns[:, 16 * k + 3 : 16 * k + 4]
        low = columns[:, 16 * k + 2 : 16 * k + 3] + columns[:, 16 * k + 4 : 16 * k + 5]
        diagonal = extra[16 * k : 16 * k + 1]
        corner = jnp.where(lower, merged, jnp.where(down == across, diagonal, turned))
        full[n * k : n * k + 128, :128] = (jnp.where(upper, merged, turned) + top).astype(BF16)
        full[n * k : n * k + 128, 128:] = (right + top).astype(BF16)
        full[n * k + 128 : n * (k + 1), :128] = (right.T + low).astype(BF16)
        full[n * k + 128 : n * (k + 1), 128:] = (corner + low).astype(BF16)


def add_increment(members, table, first_slot, packed, count, acc, left, full, state_rows):
    n = members.shape[1]
    unpack(count, packed, full)
    places = [
        pl.multiple_of(table[8, first_slot + i].astype(jnp.int32) * state_rows, state_rows)
        for i in range(CAP)
    ]
    for i in range(CAP):
        x = members[pl.ds(places[i], state_rows), :]
        for k in range(count):
            t = jnp.full((16, 128), table[k, first_slot + i], F32).astype(BF16)
            for u in range(state_rows // 16):
                for v in range(n // 128):
                    left[
                        state_rows * i + 16 * u : state_rows * i + 16 * (u + 1),
                        n * k + 128 * v : n * k + 128 * (v + 1),
                    ] = x[16 * u : 16 * (u + 1), 128 * v : 128 * (v + 1)] * t
    product = dot(left[...], full[...])
    for i in range(CAP):
        acc[pl.ds(places[i], state_rows), :] += product[state_rows * i : state_rows * (i + 1), :]


def increment_kernel(slots, start, finish, state_rows, count, *refs):
    refs = list(refs)
    members = refs.pop(0)
    before = None if start else refs.pop(0)
    items = len(slots)
    tables, packed, refs = refs[:items], refs[items : 2 * items], refs[2 * items :]
    if finish:
        out, acc = refs[:2]
        scratch = refs[2:]
    else:
        acc = refs[0]
        scratch = refs[1:]
    acc[...] = members[...].astype(F32) if start else before[...]
    for k, slot in enumerate(slots):
        left, full = scratch[2 * (k % 2) : 2 * (k % 2) + 2]
        add_increment(members, tables[k], slot, packed[k], count, acc, left, full, state_rows)
    if finish:
        out[...] = acc[...].astype(BF16)


def from_band(x, step):
    devices = range(lax.axis_size("band"))
    return lax.ppermute(x, "band", [(i + step, i) for i in devices if i + step in devices])


def from_lon(x, step):
    count = lax.axis_size("lon")
    return lax.ppermute(x, "lon", [((i + step) % count, i) for i in range(count)])


def local(members, obs_perts, innovations, lists, placement, obs_taper, state_taper):
    lon_count = lax.axis_size("lon")
    blocks, state_rows, n = members.shape
    obs_rows = obs_perts.shape[1]
    regions, list_len = lists.shape
    entries = regions * list_len

    obs = obs_perts.reshape(blocks * obs_rows, n)
    below = from_band(obs, -1)
    above = from_band(obs, 1)

    size = BAND_SLOTS * obs_rows
    pool_shape = jax.ShapeDtypeStruct((size, n), BF16)
    meta, entry_slot, obs = call(
        functools.partial(table_kernel, (lon_count, blocks)),
        (
            jax.ShapeDtypeStruct((16 + blocks, META_LANES), F32),
            jax.ShapeDtypeStruct((entries, 128), F32),
            pool_shape,
        ),
        [VMEM_SPEC] * 5,
        "tables",
        10**9,
        10**6,
    )(lists, placement.reshape(-1, 128), state_taper, innovations, obs)
    meta_w = from_lon(meta, -1)
    meta_e = from_lon(meta, 1)
    weights = call(
        functools.partial(weight_kernel, regions, list_len),
        jax.ShapeDtypeStruct((regions, CLASSES * CAP * obs_rows), F32),
        [VMEM_SPEC] * 2,
        "weights",
        10**9,
        10**6,
    )(entry_slot, jnp.swapaxes(obs_taper, 1, 2))
    below, above, weights = lax.optimization_barrier((below, above, weights))

    to_w, to_e = call(
        functools.partial(select_kernel, obs_rows),
        (pool_shape, pool_shape),
        [VMEM_SPEC] * 3 + [SMEM_SPEC] * 2,
        "select",
        10**8,
        4 * 10**6,
    )(below, obs, above, meta_w, meta_e)
    west = from_lon(to_e, -1)
    east = from_lon(to_w, 1)
    metas = jnp.concatenate([meta_w, meta, meta_e], axis=0)
    metas_below = from_band(metas, -1)
    metas_above = from_band(metas, 1)

    region_flops = 2 * n**3
    gram_own, pool = call(
        functools.partial(own_gram_kernel, obs_rows, regions),
        (jax.ShapeDtypeStruct((regions * n, n), F32), pool_shape),
        [VMEM_SPEC] * 3 + [SMEM_SPEC] + [VMEM_SPEC],
        "own_gram",
        regions * 6 * region_flops,
        5 * 10**6,
    )(below, obs, above, meta, weights)
    proj_shape = jax.ShapeDtypeStruct((regions, n), F32)
    scaled, proj_own = call(
        functools.partial(innov_kernel, obs_rows, regions),
        (jax.ShapeDtypeStruct((2 * regions, 3 * size), BF16), proj_shape),
        [VMEM_SPEC] * 6,
        "innov",
        10**8,
        2 * 10**6,
    )(meta, metas_below, metas, metas_above, weights, pool)
    mix = call(
        functools.partial(mix_kernel, 4),
        jax.ShapeDtypeStruct((regions * (n + 16), 128), BF16),
        [VMEM_SPEC] * 6,
        "mixing",
        regions * 24 * region_flops,
        4 * 10**6,
        [pltpu.VMEM(proj_shape.shape, F32)],
    )(west, east, weights, gram_own, scaled, proj_own)

    arrived = {}
    for band, packed in ((0, mix), (-1, from_band(mix, -1)), (1, from_band(mix, 1))):
        arrived[0, band] = packed
        for lon in (-1, 1):
            arrived[lon, band] = from_lon(packed, lon)

    stacked = {-1: metas_below, 0: metas, 1: metas_above}
    rows = 16 + blocks

    def table(lon, band):
        return stacked[band][rows * (lon + 1) : rows * (lon + 1) + 16]

    def slots(lon, band):
        return CAP * (CLASSES - 1 - ((lon + 1) * 3 + band + 1))

    flat = members.reshape(blocks * state_rows, n)
    acc_shape = jax.ShapeDtypeStruct((blocks * state_rows, n), F32)
    scratch = [
        pltpu.VMEM((CAP * state_rows, regions * n), BF16),
        pltpu.VMEM((regions * n, n), BF16),
    ] * 2

    def increments(acc, groups, finish, name):
        start = acc is None
        kernel = functools.partial(
            increment_kernel, [slots(*g) for g in groups], start, finish, state_rows, regions
        )
        return call(
            kernel,
            jax.ShapeDtypeStruct(acc_shape.shape, BF16) if finish else acc_shape,
            [VMEM_SPEC] * (1 if start else 2)
            + [SMEM_SPEC] * len(groups)
            + [VMEM_SPEC] * len(groups),
            name,
            len(groups) * 3 * regions * region_flops,
            6 * 10**6,
            ([pltpu.VMEM(acc_shape.shape, F32)] if finish else []) + scratch,
        )(
            *([flat] if start else [flat, acc]),
            *[table(*g) for g in groups],
            *[arrived[g] for g in groups],
        )

    acc = increments(None, [(0, 0), (0, -1), (0, 1), (-1, 0), (1, 0)], False, "inner")
    acc = increments(acc, [(-1, -1), (1, -1)], False, "outer")
    acc = increments(acc, [(-1, 1), (1, 1)], True, "finish")
    return acc.reshape(members.shape)


def solution(mesh):
    in_specs = (
        P(("band", "lon"), None, None),
        P(("band", "lon"), None, None),
        P(("band", "lon"), None),
        P(("band", "lon"), None),
        P(),
        P(("band", "lon"), None, None),
        P(("band", "lon"), None),
    )
    out_specs = P(("band", "lon"), None, None)
    return jax.shard_map(local, mesh=mesh, in_specs=in_specs, out_specs=out_specs, check_vma=False)
```

```python
import functools

import jax
import jax.numpy as jnp
from jax import lax
from jax.experimental import pallas as pl
from jax.experimental.pallas import tpu as pltpu
from jax.sharding import PartitionSpec as P

NS_ITERS = 5
CAP = 16
SELF, FIRST, SECOND = 0, 1, 2
CLASSES = 9
BAND_SLOTS = 3 * CAP
CLASS_STRIDE = 64
KEYS = 640
META_LANES = 256
META_ROWS = 16
BLOCK_ROW = 8
INNOV_ROW = 9

F32 = jnp.float32
BF16 = jnp.bfloat16
VMEM_SPEC = pl.BlockSpec(memory_space=pltpu.VMEM)
SMEM_SPEC = pl.BlockSpec(memory_space=pltpu.SMEM)


def dot(a, b):
    return jnp.dot(a, b, preferred_element_type=F32)


def call(kernel, outs, in_specs, name, flops, bytes_accessed, scratch=(), aliases=None):
    return pl.pallas_call(
        kernel,
        out_shape=outs,
        in_specs=in_specs,
        out_specs=jax.tree.map(lambda _: VMEM_SPEC, outs),
        scratch_shapes=list(scratch),
        input_output_aliases=aliases or {},
        compiler_params=pltpu.CompilerParams(vmem_limit_bytes=40 * 1024 * 1024),
        cost_estimate=pl.CostEstimate(
            flops=flops, bytes_accessed=bytes_accessed, transcendentals=0
        ),
        name=name,
    )


def fold(x, width):
    per = META_LANES // width
    sub = lax.broadcasted_iota(jnp.int32, (per, META_LANES), 0)
    which = lax.broadcasted_iota(jnp.int32, (per, META_LANES), 1) // width
    return jnp.concatenate(
        [
            jnp.sum(jnp.where(sub == which, x[i : i + per], 0.0), axis=0, keepdims=True)
            for i in range(0, x.shape[0], per)
        ],
        axis=0,
    )


def table_kernel(shape, lists, placement, state, innov, obs, meta, entry_slot, obs_copy):
    lon_count, blocks = shape
    regions, list_len = lists.shape
    entries = regions * list_len
    obs_rows = innov.shape[1]
    obs_copy[...] = obs[...]
    p = lax.broadcasted_iota(jnp.int32, (obs_rows, META_LANES), 0)
    q = lax.broadcasted_iota(jnp.int32, (obs_rows, META_LANES), 1) % obs_rows
    repeated = dot(innov[...], jnp.where(p == q, 1.0, 0.0).astype(BF16))
    meta[...] = jnp.zeros_like(meta)
    folded = fold(repeated, obs_rows)
    meta[INNOV_ROW : INNOV_ROW + folded.shape[0], :] = folded

    def columns(x):
        t = x.T
        return jnp.concatenate(
            [jnp.broadcast_to(t[:, r : r + 1], (list_len, 128)) for r in range(regions)], axis=0
        )

    lane = lax.broadcasted_iota(jnp.int32, (1, 128), 1).astype(F32)
    ones = jnp.ones((128, 128), BF16)
    ids = columns(lists[...].astype(F32))
    line = jnp.floor(ids * (1.0 / 128.0))
    table_rows = placement.shape[0]
    line_hot = jnp.where(line == lane, 1.0, 0.0).astype(BF16)[:, :table_rows]
    at = lane == ids - 128.0 * line
    places = placement[...].astype(F32)
    high = jnp.floor(places * (1.0 / 64.0))

    def look(part):
        found = dot(line_hot, part.astype(BF16))
        return dot(jnp.where(at, found, 0.0).astype(BF16), ones)

    row = 64.0 * look(high) + look(places - 64.0 * high)
    holder = jnp.floor((row + 0.5) * (1.0 / blocks))
    inside = row - blocks * holder
    holder_band = jnp.floor((holder + 0.5) * (1.0 / lon_count))
    band_here = lax.axis_index("band")
    lon_here = lax.axis_index("lon")
    band_step = holder_band - band_here.astype(F32)
    lon_step = holder - lon_count * holder_band - lon_here.astype(F32)
    half = lon_count // 2
    lon_step = jnp.where(lon_step < -half, lon_step + lon_count, lon_step)
    lon_step = jnp.where(lon_step > half, lon_step - lon_count, lon_step)
    band_turn = band_step * (1 - 2 * (band_here % 2)).astype(F32)
    lon_turn = lon_step * (2 * (lon_here % 2) - 1).astype(F32)
    band_place = jnp.where(band_turn == 0.0, 0.0, jnp.where(band_turn > 0.0, 1.0, 2.0))
    lon_place = jnp.where(lon_turn == 0.0, 0.0, jnp.where(lon_turn > 0.0, 1.0, 2.0))
    key = (lon_place * 3.0 + band_place) * CLASS_STRIDE + inside

    hot = jnp.concatenate(
        [jnp.where(key == lane + 128.0 * c, 1.0, 0.0) for c in range(KEYS // 128)], axis=1
    ).astype(BF16)
    counts = lax.dot_general(
        hot,
        jnp.ones((entries, 128), BF16),
        (((0,), (0,)), ((), ())),
        preferred_element_type=F32,
    )
    present = jnp.minimum(counts, 1.0)
    down = lax.broadcasted_iota(jnp.int32, (KEYS, KEYS), 0)
    across = lax.broadcasted_iota(jnp.int32, (KEYS, KEYS), 1)
    before = (across < down) & (across // CLASS_STRIDE == down // CLASS_STRIDE)
    rank = dot(jnp.where(before, 1.0, 0.0).astype(BF16), present.astype(BF16))
    key_id = lax.broadcasted_iota(jnp.int32, (KEYS, 128), 0)
    slot = rank + (CAP * (key_id // CLASS_STRIDE)).astype(F32)
    block = (key_id % CLASS_STRIDE).astype(F32)
    slots = dot(hot, slot.astype(BF16))
    entry_slot[...] = slots
    tapers = columns(state[...])
    for c in range(2):
        match = (slot == lane + 128.0 * c) & (present > 0.0)
        rows = jnp.sum(jnp.where(match, block, 0.0), axis=0, keepdims=True)
        meta[BLOCK_ROW : BLOCK_ROW + 1, 128 * c : 128 * (c + 1)] = rows
        hit = jnp.where(slots == lane + 128.0 * c, tapers, 0.0)
        for r in range(regions):
            meta[r : r + 1, 128 * c : 128 * (c + 1)] = jnp.sum(
                hit[r * list_len : (r + 1) * list_len], axis=0, keepdims=True
            )


def weight_kernel(regions, list_len, entry_slot, taper, weights):
    obs_rows = taper.shape[1]
    group = (lax.broadcasted_iota(jnp.int32, (1, 128), 1) // obs_rows).astype(F32)
    p = lax.broadcasted_iota(jnp.int32, (obs_rows, 128), 0)
    q = lax.broadcasted_iota(jnp.int32, (obs_rows, 128), 1) % obs_rows
    spread = jnp.where(p == q, 1.0, 0.0).astype(BF16)

    def across(x):
        return lax.dot_general(
            x, spread, (((0,), (0,)), ((), ())), preferred_element_type=F32
        )

    for r in range(regions):
        mine = entry_slot[r * list_len : (r + 1) * list_len, :]
        high = taper[r].astype(BF16)
        low = (taper[r] - high.astype(F32)).astype(BF16)
        w = across(high) + across(low)
        for c in range(CLASSES * CAP // 4):
            hit = mine == group + 4.0 * c
            weights[r : r + 1, 128 * c : 128 * (c + 1)] = jnp.sum(
                jnp.where(hit, w, 0.0), axis=0, keepdims=True
            )


def gather_blocks(sources, table, first_slot, obs_rows, out):
    for k, source in enumerate(sources):
        for i in range(CAP):
            block = table[BLOCK_ROW, first_slot + CAP * k + i].astype(jnp.int32)
            at = pl.multiple_of(block * obs_rows, obs_rows)
            to = (CAP * k + i) * obs_rows
            out[to : to + obs_rows, :] = source[pl.ds(at, obs_rows), :]


def select_kernel(obs_rows, obs, obs_1, obs_2, table_1, table_2, to_1, to_2):
    sources = (obs, obs_1, obs_2)
    gather_blocks(sources, table_1, FIRST * BAND_SLOTS, obs_rows, to_1)
    gather_blocks(sources, table_2, SECOND * BAND_SLOTS, obs_rows, to_2)


def transposed(y):
    return jnp.concatenate(
        [y[256 * c : 256 * (c + 1)].astype(F32).T.astype(BF16) for c in range(y.shape[0] // 256)],
        axis=1,
    )


def own_gram_kernel(obs_rows, regions, obs, obs_1, obs_2, table, weights, gram, pool):
    gather_blocks((obs, obs_1, obs_2), table, SELF * BAND_SLOTS, obs_rows, pool)
    y = pool[...]
    y_t = transposed(y)
    first = SELF * BAND_SLOTS * obs_rows
    w16 = weights[:, first : first + y.shape[0]].astype(BF16)
    for r in range(regions):
        gram[256 * r : 256 * (r + 1), :] = dot(y_t * w16[r : r + 1, :], y)


def innov_kernel(obs_rows, regions, blocks, metas, metas_1, metas_2, weights, pool, scaled, proj):
    down = lax.broadcasted_iota(jnp.int32, (blocks, META_LANES), 0).astype(F32)
    mine = metas[META_ROWS * SELF + BLOCK_ROW : META_ROWS * SELF + BLOCK_ROW + 1, :]
    hot = jnp.where(down == mine, 1.0, 0.0).T.astype(BF16)
    per = META_LANES // obs_rows
    sub = lax.broadcasted_iota(jnp.int32, (per, META_LANES), 0)
    which = lax.broadcasted_iota(jnp.int32, (per, META_LANES), 1) // obs_rows
    picked = []
    for n in range(CLASSES):
        source = (metas, metas_1, metas_2)[n % 3]
        base = META_ROWS * (n // 3) + INNOV_ROW
        rows = [
            jnp.where(sub == which, source[base + i : base + i + 1, :], 0.0)
            for i in range(blocks // per)
        ]
        picked.append(dot(hot[CAP * n : CAP * (n + 1)], jnp.concatenate(rows, axis=0).astype(BF16)))
    p = lax.broadcasted_iota(jnp.int32, (META_LANES, META_LANES), 0) % obs_rows
    q = lax.broadcasted_iota(jnp.int32, (META_LANES, META_LANES), 1) % obs_rows
    spread = jnp.where(p == q, 1.0, 0.0).astype(BF16)
    repeated = dot(jnp.concatenate(picked, axis=0).astype(BF16), spread)
    folded = fold(repeated, obs_rows)
    lanes = jnp.concatenate([folded[i : i + 1] for i in range(folded.shape[0])], axis=1)
    wd = weights[...] * lanes
    high = wd.astype(BF16)
    both = jnp.concatenate([high.astype(F32), wd - high.astype(F32)], axis=0).astype(BF16)
    scaled[...] = both
    first = SELF * BAND_SLOTS * obs_rows
    part = dot(both[:, first : first + pool.shape[0]], pool[...])
    proj[...] = part[:regions] + part[regions:]


def quarters(x):
    return x[:128, :128], x[:128, 128:], x[128:, :128], x[128:, 128:]


def add_diagonal(x, d, eye):
    q = quarters(x)
    top = jnp.concatenate([q[0] + d * eye, q[1]], axis=1)
    low = jnp.concatenate([q[2], q[3] + d * eye], axis=1)
    return jnp.concatenate([top, low], axis=0)


def trace(x, eye):
    q = quarters(x)
    both = (q[0] + q[3]) * eye
    return jnp.sum(jnp.sum(both, axis=0, keepdims=True), axis=1, keepdims=True)


def roots(grams, proj_rows, eye, ensemble):
    each = range(len(grams))
    base = ensemble - 1.0
    scale = [
        base
        + jnp.max(jnp.sum(jnp.abs(grams[i]), axis=0, keepdims=True), axis=1, keepdims=True)
        for i in each
    ]
    inverse = [1.0 / scale[i] for i in each]
    mean = [trace(grams[i], eye) * (1.0 / ensemble) for i in each]
    u = [
        add_diagonal(grams[i] * (-0.5 * inverse[i]), 0.5 * inverse[i] * mean[i], eye)
        for i in each
    ]
    c = [1.0 - (base + mean[i]) * inverse[i] for i in each]
    a = [1.0 + 0.5 * c[i] for i in each]
    g = u
    ub = [u[i].astype(BF16) for i in each]
    gb = ub
    for step in range(NS_ITERS - 1):
        u2 = [dot(ub[i], ub[i]) for i in each]
        w = [((1.5 + 1.5 * c[i]) * u[i] + u2[i]).astype(BF16) for i in each]
        u3 = [dot(ub[i], w[i]) for i in each]
        u = [(1.5 * c[i] + 0.75 * c[i] * c[i]) * u[i] + u3[i] for i in each]
        c = [(0.75 + 0.25 * c[i]) * c[i] * c[i] for i in each]
        ub = [u[i].astype(BF16) for i in each]
        ug = [dot(ub[i], gb[i]) for i in each]
        g = [(1.0 + 0.5 * c[i]) * g[i] + a[i] * u[i] + ug[i] for i in each]
        gb = [g[i].astype(BF16) for i in each]
        a = [a[i] * (1.0 + 0.5 * c[i]) for i in each]
    first = lax.broadcasted_iota(jnp.int32, (16, ensemble), 0) < 8

    def times(i, v):
        high = v.astype(BF16).astype(F32)
        stacked = jnp.where(first, high, v - high).astype(BF16)
        q = dot(stacked, gb[i])
        return a[i] * v + q[0:1] + q[8:9]

    half = [times(i, proj_rows[i]) for i in each]
    wbar = [times(i, half[i]) * inverse[i] for i in each]
    factor = [lax.sqrt(base * inverse[i]) for i in each]
    return [(factor[i], factor[i] * a[i] - 1.0, g[i]) for i in each], wbar


def pack(matrix, wbar, eye, upper):
    factor, diagonal, g = matrix
    q = quarters(g)
    left = factor * q[0] + diagonal * eye
    right = factor * q[1]
    corner = factor * q[3] + diagonal * eye
    merged = jnp.where(upper, left, corner)
    high = wbar.astype(BF16).astype(F32)
    low = wbar - high
    rows = [
        jnp.sum(corner * eye, axis=0, keepdims=True),
        high[:, :128],
        high[:, 128:],
        low[:, :128],
        low[:, 128:],
    ]
    down = lax.broadcasted_iota(jnp.int32, (16, 128), 0)
    extra = jnp.zeros((16, 128), F32)
    for k, r in enumerate(rows):
        extra = jnp.where(down == k, r, extra)
    return right.astype(BF16), merged.astype(BF16), extra.astype(BF16)


def mix_regions(first, count, gram, proj, packed):
    n = 256
    extras = n * proj.shape[0]
    down = lax.broadcasted_iota(jnp.int32, (128, 128), 0)
    across = lax.broadcasted_iota(jnp.int32, (128, 128), 1)
    eye = jnp.where(down == across, 1.0, 0.0)
    some = range(first, first + count)
    matrices, weights = roots(
        [gram[r - first] for r in some], [proj[r : r + 1, :] for r in some], eye, n
    )
    for k, r in enumerate(some):
        right, merged, extra = pack(matrices[k], weights[k], eye, down <= across)
        packed[n * r : n * r + 128, :] = right
        packed[n * r + 128 : n * (r + 1), :] = merged
        packed[extras + 16 * r : extras + 16 * (r + 1), :] = extra


def grams_of(first, count, gram_own, weights, parts):
    out = []
    for r in range(first, first + count):
        total_r = gram_own[256 * r : 256 * (r + 1), :]
        for y, y_t, lane in parts:
            w16 = weights[r : r + 1, lane : lane + y.shape[0]].astype(BF16)
            total_r = total_r + dot(y_t * w16, y)
        out.append(total_r)
    return out


def mix_kernel(together, lanes, *refs):
    pools, refs = refs[: len(lanes)], refs[len(lanes) :]
    weights, gram_own, scaled, proj_own, packed, proj = refs
    regions = proj.shape[0]
    part = sum(
        dot(scaled[:, lane : lane + y.shape[0]], y[...]) for y, lane in zip(pools, lanes)
    )
    proj[...] = proj_own[...] + part[:regions] + part[regions:]
    parts = [(y[...], transposed(y[...]), lane) for y, lane in zip(pools, lanes)]
    for first in range(0, regions, together):
        grams = grams_of(first, together, gram_own, weights, parts)
        mix_regions(first, together, grams, proj, packed)


def unpack(count, packed, full):
    n = 256
    down = lax.broadcasted_iota(jnp.int32, (128, 128), 0)
    across = lax.broadcasted_iota(jnp.int32, (128, 128), 1)
    upper = down <= across
    lower = down > across
    extra = packed[n * count : (n + 16) * count, :].astype(F32)
    columns = extra.T.astype(BF16)

    def spread(k):
        return dot(columns, jnp.where((down == k) | (down == k + 2), 1.0, 0.0).astype(BF16))

    for k in range(count):
        right = packed[n * k : n * k + 128, :].astype(F32)
        merged = packed[n * k + 128 : n * (k + 1), :].astype(F32)
        turned = merged.T
        top = spread(16 * k + 1)
        low = spread(16 * k + 2)
        diagonal = extra[16 * k : 16 * k + 1]
        corner = jnp.where(lower, merged, jnp.where(down == across, diagonal, turned))
        full[n * k : n * k + 128, :128] = (jnp.where(upper, merged, turned) + top).astype(BF16)
        full[n * k : n * k + 128, 128:] = (right + top).astype(BF16)
        full[n * k + 128 : n * (k + 1), :128] = (right.T + low).astype(BF16)
        full[n * k + 128 : n * (k + 1), 128:] = (corner + low).astype(BF16)


def add_increment(members, table, first_slot, packed, count, acc, left, full, state_rows):
    n = members.shape[1]
    unpack(count, packed, full)
    places = [
        pl.multiple_of(table[BLOCK_ROW, first_slot + i].astype(jnp.int32) * state_rows, state_rows)
        for i in range(CAP)
    ]
    for i in range(CAP):
        x = members[pl.ds(places[i], state_rows), :]
        for k in range(count):
            t = jnp.full((16, 128), table[k, first_slot + i], F32).astype(BF16)
            for u in range(state_rows // 16):
                for v in range(n // 128):
                    left[
                        state_rows * i + 16 * u : state_rows * i + 16 * (u + 1),
                        n * k + 128 * v : n * k + 128 * (v + 1),
                    ] = x[16 * u : 16 * (u + 1), 128 * v : 128 * (v + 1)] * t
    product = dot(left[...], full[...])
    for i in range(CAP):
        acc[pl.ds(places[i], state_rows), :] += product[state_rows * i : state_rows * (i + 1), :]


def increment_kernel(slots, halves, start, finish, state_rows, count, *refs):
    refs = list(refs)
    members = refs.pop(0)
    before = None if start else refs.pop(0)
    items = len(slots)
    tables, packed, refs = refs[:items], refs[items : 2 * items], refs[2 * items :]
    rows = count * (members.shape[1] + 16)
    if finish:
        out, acc = refs[:2]
        scratch = refs[2:]
    else:
        acc = refs[0]
        scratch = refs[1:]
    acc[...] = members[...].astype(F32) if start else before[...]
    for k, slot in enumerate(slots):
        left, full = scratch[2 * (k % 2) : 2 * (k % 2) + 2]
        mixes = packed[k].at[rows * halves[k] : rows * (halves[k] + 1), :]
        add_increment(members, tables[k], slot, mixes, count, acc, left, full, state_rows)
    if finish:
        out[...] = acc[...].astype(BF16)


def from_band(x, place):
    count = lax.axis_size("band")
    step = 1 if place == FIRST else -1
    pairs = [(i + step * (1 - 2 * (i % 2)), i) for i in range(count)]
    return lax.ppermute(x, "band", [(j, i) for j, i in pairs if 0 <= j < count])


def from_lon(x, place):
    count = lax.axis_size("lon")
    step = -1 if place == FIRST else 1
    return lax.ppermute(
        x, "lon", [((i + step * (1 - 2 * (i % 2))) % count, i) for i in range(count)]
    )


def local(members, obs_perts, innovations, lists, placement, obs_taper, state_taper):
    lon_count = lax.axis_size("lon")
    blocks, state_rows, n = members.shape
    obs_rows = obs_perts.shape[1]
    regions, list_len = lists.shape
    entries = regions * list_len

    obs = obs_perts.reshape(blocks * obs_rows, n)
    obs_1 = from_band(obs, FIRST)
    obs_2 = from_band(obs, SECOND)

    meta, entry_slot, obs = call(
        functools.partial(table_kernel, (lon_count, blocks)),
        (
            jax.ShapeDtypeStruct((META_ROWS, META_LANES), F32),
            jax.ShapeDtypeStruct((entries, 128), F32),
            jax.ShapeDtypeStruct(obs.shape, BF16),
        ),
        [VMEM_SPEC] * 5,
        "tables",
        10**9,
        10**6,
    )(lists, placement.reshape(-1, 128), state_taper, innovations, obs)
    meta_1 = from_lon(meta, FIRST)
    meta_2 = from_lon(meta, SECOND)

    weights = call(
        functools.partial(weight_kernel, regions, list_len),
        jax.ShapeDtypeStruct((regions, CLASSES * CAP * obs_rows), F32),
        [VMEM_SPEC] * 2,
        "weights",
        10**9,
        10**6,
    )(entry_slot, jnp.swapaxes(obs_taper, 1, 2))
    obs_1, obs_2, weights = lax.optimization_barrier((obs_1, obs_2, weights))
    size = BAND_SLOTS * obs_rows
    pool_shape = jax.ShapeDtypeStruct((size, n), BF16)
    to_1, to_2 = call(
        functools.partial(select_kernel, obs_rows),
        (pool_shape, pool_shape),
        [VMEM_SPEC] * 3 + [SMEM_SPEC] * 2,
        "select",
        10**8,
        4 * 10**6,
    )(obs, obs_1, obs_2, meta_1, meta_2)
    pool_1 = from_lon(to_1, FIRST)
    pool_2 = from_lon(to_2, SECOND)
    metas = jnp.concatenate([meta, meta_1, meta_2], axis=0)
    metas_1 = from_band(metas, FIRST)
    metas_2 = from_band(metas, SECOND)

    region_flops = 2 * n**3
    gram_own, pool = call(
        functools.partial(own_gram_kernel, obs_rows, regions),
        (
            jax.ShapeDtypeStruct((regions * n, n), F32),
            pool_shape,
        ),
        [VMEM_SPEC] * 3 + [SMEM_SPEC] + [VMEM_SPEC],
        "own_gram",
        regions * 6 * region_flops,
        5 * 10**6,
    )(obs, obs_1, obs_2, meta, weights)
    proj_shape = jax.ShapeDtypeStruct((regions, n), F32)
    scaled, proj_own = call(
        functools.partial(innov_kernel, obs_rows, regions, blocks),
        (jax.ShapeDtypeStruct((2 * regions, 3 * size), BF16), proj_shape),
        [VMEM_SPEC] * 5,
        "innov",
        10**8,
        2 * 10**6,
    )(metas, metas_1, metas_2, weights, pool)
    mix = call(
        functools.partial(mix_kernel, 4, [FIRST * size, SECOND * size]),
        jax.ShapeDtypeStruct((regions * (n + 16), 128), BF16),
        [VMEM_SPEC] * 6,
        "mixing",
        regions * 24 * region_flops,
        4 * 10**6,
        [pltpu.VMEM(proj_shape.shape, F32)],
    )(pool_1, pool_2, weights, gram_own, scaled, proj_own)

    stacked = (metas, metas_1, metas_2)

    def table(lon, band):
        return stacked[band][META_ROWS * lon : META_ROWS * (lon + 1)]

    def slots(lon, band):
        return CAP * (lon * 3 + band)

    flat = members.reshape(blocks * state_rows, n)
    acc_shape = jax.ShapeDtypeStruct((blocks * state_rows, n), F32)
    scratch = [
        pltpu.VMEM((CAP * state_rows, regions * n), BF16),
        pltpu.VMEM((regions * n, n), BF16),
    ] * 2

    def increments(acc, groups, finish, name):
        start = acc is None
        kernel = functools.partial(
            increment_kernel,
            [slots(*g) for g in groups],
            [arrived[g][1] for g in groups],
            start,
            finish,
            state_rows,
            regions,
        )
        return call(
            kernel,
            jax.ShapeDtypeStruct(acc_shape.shape, BF16) if finish else acc_shape,
            [VMEM_SPEC] * (1 if start else 2)
            + [SMEM_SPEC] * len(groups)
            + [VMEM_SPEC] * len(groups),
            name,
            len(groups) * 3 * regions * region_flops,
            6 * 10**6,
            ([pltpu.VMEM(acc_shape.shape, F32)] if finish else []) + scratch,
        )(
            *([flat] if start else [flat, acc]),
            *[table(*g) for g in groups],
            *[arrived[g][0] for g in groups],
        )

    arrived = {(SELF, SELF): (mix, 0)}
    for lon in (FIRST, SECOND):
        arrived[lon, SELF] = (from_lon(mix, lon), 0)
    mix_1, mix_2 = from_band(mix, FIRST), from_band(mix, SECOND)
    acc = increments(None, [(SELF, SELF), (SECOND, SELF)], False, "own")
    acc, mix_1, mix_2, near = lax.optimization_barrier(
        (acc, mix_1, mix_2, arrived[FIRST, SELF][0])
    )
    arrived[FIRST, SELF] = (near, 0)
    both = jnp.concatenate([mix_1, mix_2], axis=0)
    arrived[SELF, FIRST], arrived[SELF, SECOND] = (mix_1, 0), (mix_2, 0)
    for lon in (FIRST, SECOND):
        there = from_lon(both, lon)
        arrived[lon, FIRST], arrived[lon, SECOND] = (there, 0), (there, 1)
    acc = increments(acc, [(SELF, FIRST), (SELF, SECOND), (FIRST, SELF)], False, "inner")
    acc = increments(acc, [(SECOND, FIRST), (SECOND, SECOND)], False, "outer")
    acc = increments(acc, [(FIRST, FIRST), (FIRST, SECOND)], True, "finish")
    return acc.reshape(members.shape)


def solution(mesh):
    in_specs = (
        P(("band", "lon"), None, None),
        P(("band", "lon"), None, None),
        P(("band", "lon"), None),
        P(("band", "lon"), None),
        P(),
        P(("band", "lon"), None, None),
        P(("band", "lon"), None),
    )
    out_specs = P(("band", "lon"), None, None)
    return jax.shard_map(local, mesh=mesh, in_specs=in_specs, out_specs=out_specs, check_vma=False)
```

```python
import functools

import jax
import jax.numpy as jnp
from jax import lax
from jax.experimental import pallas as pl
from jax.experimental.pallas import tpu as pltpu
from jax.sharding import PartitionSpec as P

NS_ITERS = 5
CAP = 16
SELF, FIRST, SECOND = 0, 1, 2
CLASSES = 9
BAND_SLOTS = 3 * CAP
CLASS_STRIDE = 64
KEYS = 640
META_LANES = 256
META_ROWS = 16
BLOCK_ROW = 8
INNOV_ROW = 9

F32 = jnp.float32
BF16 = jnp.bfloat16
VMEM_SPEC = pl.BlockSpec(memory_space=pltpu.VMEM)
SMEM_SPEC = pl.BlockSpec(memory_space=pltpu.SMEM)
HBM_SPEC = pl.BlockSpec(memory_space=pltpu.HBM)


def dot(a, b):
    return jnp.dot(a, b, preferred_element_type=F32)


def call(kernel, outs, in_specs, name, flops, bytes_accessed, scratch=(), aliases=None):
    return pl.pallas_call(
        kernel,
        out_shape=outs,
        in_specs=in_specs,
        out_specs=jax.tree.map(lambda _: VMEM_SPEC, outs),
        scratch_shapes=list(scratch),
        input_output_aliases=aliases or {},
        compiler_params=pltpu.CompilerParams(vmem_limit_bytes=40 * 1024 * 1024),
        cost_estimate=pl.CostEstimate(
            flops=flops, bytes_accessed=bytes_accessed, transcendentals=0
        ),
        name=name,
    )


def fold(x, width):
    per = META_LANES // width
    sub = lax.broadcasted_iota(jnp.int32, (per, META_LANES), 0)
    which = lax.broadcasted_iota(jnp.int32, (per, META_LANES), 1) // width
    return jnp.concatenate(
        [
            jnp.sum(jnp.where(sub == which, x[i : i + per], 0.0), axis=0, keepdims=True)
            for i in range(0, x.shape[0], per)
        ],
        axis=0,
    )


def table_kernel(shape, *refs):
    lon_count, blocks = shape
    sources, (meta, entry_slot, obs), copies, sems = refs[:5], refs[5:8], refs[8:12], refs[12]
    transfers = [
        pltpu.make_async_copy(source, to, sems.at[k])
        for k, (source, to) in enumerate(zip(sources, copies + (obs,)))
    ]
    for transfer in transfers:
        transfer.start()
    for transfer in transfers[:-1]:
        transfer.wait()
    lists, placement, state, innov = copies
    regions, list_len = lists.shape
    entries = regions * list_len
    obs_rows = innov.shape[1]
    p = lax.broadcasted_iota(jnp.int32, (obs_rows, META_LANES), 0)
    q = lax.broadcasted_iota(jnp.int32, (obs_rows, META_LANES), 1) % obs_rows
    repeated = dot(innov[...], jnp.where(p == q, 1.0, 0.0).astype(BF16))
    meta[...] = jnp.zeros_like(meta)
    folded = fold(repeated, obs_rows)
    meta[INNOV_ROW : INNOV_ROW + folded.shape[0], :] = folded

    def columns(x):
        t = x.T
        return jnp.concatenate(
            [jnp.broadcast_to(t[:, r : r + 1], (list_len, 128)) for r in range(regions)], axis=0
        )

    lane = lax.broadcasted_iota(jnp.int32, (1, 128), 1).astype(F32)
    ones = jnp.ones((128, 128), BF16)
    ids = columns(lists[...].astype(F32))
    line = jnp.floor(ids * (1.0 / 128.0))
    table_rows = placement.shape[0]
    line_hot = jnp.where(line == lane, 1.0, 0.0).astype(BF16)[:, :table_rows]
    at = lane == ids - 128.0 * line
    places = placement[...].astype(F32)
    high = jnp.floor(places * (1.0 / 64.0))

    def look(part):
        found = dot(line_hot, part.astype(BF16))
        return dot(jnp.where(at, found, 0.0).astype(BF16), ones)

    row = 64.0 * look(high) + look(places - 64.0 * high)
    holder = jnp.floor((row + 0.5) * (1.0 / blocks))
    inside = row - blocks * holder
    holder_band = jnp.floor((holder + 0.5) * (1.0 / lon_count))
    band_here = lax.axis_index("band")
    lon_here = lax.axis_index("lon")
    band_step = holder_band - band_here.astype(F32)
    lon_step = holder - lon_count * holder_band - lon_here.astype(F32)
    half = lon_count // 2
    lon_step = jnp.where(lon_step < -half, lon_step + lon_count, lon_step)
    lon_step = jnp.where(lon_step > half, lon_step - lon_count, lon_step)
    band_turn = band_step * (1 - 2 * (band_here % 2)).astype(F32)
    lon_turn = lon_step * (2 * (lon_here % 2) - 1).astype(F32)
    band_place = jnp.where(band_turn == 0.0, 0.0, jnp.where(band_turn > 0.0, 1.0, 2.0))
    lon_place = jnp.where(lon_turn == 0.0, 0.0, jnp.where(lon_turn > 0.0, 1.0, 2.0))
    key = (lon_place * 3.0 + band_place) * CLASS_STRIDE + inside

    hot = jnp.concatenate(
        [jnp.where(key == lane + 128.0 * c, 1.0, 0.0) for c in range(KEYS // 128)], axis=1
    ).astype(BF16)
    counts = lax.dot_general(
        hot,
        jnp.ones((entries, 128), BF16),
        (((0,), (0,)), ((), ())),
        preferred_element_type=F32,
    )
    present = jnp.minimum(counts, 1.0)
    down = lax.broadcasted_iota(jnp.int32, (KEYS, KEYS), 0)
    across = lax.broadcasted_iota(jnp.int32, (KEYS, KEYS), 1)
    before = (across < down) & (across // CLASS_STRIDE == down // CLASS_STRIDE)
    rank = dot(jnp.where(before, 1.0, 0.0).astype(BF16), present.astype(BF16))
    key_id = lax.broadcasted_iota(jnp.int32, (KEYS, 128), 0)
    slot = rank + (CAP * (key_id // CLASS_STRIDE)).astype(F32)
    block = (key_id % CLASS_STRIDE).astype(F32)
    slots = dot(hot, slot.astype(BF16))
    entry_slot[...] = slots
    tapers = columns(state[...])
    for c in range(2):
        match = (slot == lane + 128.0 * c) & (present > 0.0)
        rows = jnp.sum(jnp.where(match, block, 0.0), axis=0, keepdims=True)
        meta[BLOCK_ROW : BLOCK_ROW + 1, 128 * c : 128 * (c + 1)] = rows
        hit = jnp.where(slots == lane + 128.0 * c, tapers, 0.0)
        for r in range(regions):
            meta[r : r + 1, 128 * c : 128 * (c + 1)] = jnp.sum(
                hit[r * list_len : (r + 1) * list_len], axis=0, keepdims=True
            )
    transfers[-1].wait()


def weight_kernel(regions, list_len, entry_slot, taper, weights):
    obs_rows = taper.shape[1]
    group = (lax.broadcasted_iota(jnp.int32, (1, 128), 1) // obs_rows).astype(F32)
    p = lax.broadcasted_iota(jnp.int32, (obs_rows, 128), 0)
    q = lax.broadcasted_iota(jnp.int32, (obs_rows, 128), 1) % obs_rows
    spread = jnp.where(p == q, 1.0, 0.0).astype(BF16)

    def across(x):
        return lax.dot_general(
            x, spread, (((0,), (0,)), ((), ())), preferred_element_type=F32
        )

    for r in range(regions):
        mine = entry_slot[r * list_len : (r + 1) * list_len, :]
        high = taper[r].astype(BF16)
        low = (taper[r] - high.astype(F32)).astype(BF16)
        w = across(high) + across(low)
        for c in range(CLASSES * CAP // 4):
            hit = mine == group + 4.0 * c
            weights[r : r + 1, 128 * c : 128 * (c + 1)] = jnp.sum(
                jnp.where(hit, w, 0.0), axis=0, keepdims=True
            )


def gather_blocks(sources, table, first_slot, obs_rows, out):
    for k, source in enumerate(sources):
        for i in range(CAP):
            block = table[BLOCK_ROW, first_slot + CAP * k + i].astype(jnp.int32)
            at = pl.multiple_of(block * obs_rows, obs_rows)
            to = (CAP * k + i) * obs_rows
            out[to : to + obs_rows, :] = source[pl.ds(at, obs_rows), :]


def select_kernel(obs_rows, obs, obs_1, obs_2, table_1, table_2, to_1, to_2):
    sources = (obs, obs_1, obs_2)
    gather_blocks(sources, table_1, FIRST * BAND_SLOTS, obs_rows, to_1)
    gather_blocks(sources, table_2, SECOND * BAND_SLOTS, obs_rows, to_2)


def transposed(y):
    return jnp.concatenate(
        [y[256 * c : 256 * (c + 1)].astype(F32).T.astype(BF16) for c in range(y.shape[0] // 256)],
        axis=1,
    )


def near_gram_kernel(obs_rows, regions, obs, obs_1, obs_2, pool_2, table, weights, gram, pool):
    gather_blocks((obs, obs_1, obs_2), table, SELF * BAND_SLOTS, obs_rows, pool)
    size = pool.shape[0]
    parts = [(y[...], transposed(y[...]), at * size) for y, at in ((pool, SELF), (pool_2, SECOND))]
    for r in range(regions):
        gram[256 * r : 256 * (r + 1), :] = gram_of(r, weights, parts)


def gram_of(r, weights, parts):
    products = [
        dot(y_t * weights[r : r + 1, lane : lane + y.shape[0]].astype(BF16), y)
        for y, y_t, lane in parts
    ]
    return sum(products[1:], products[0])


def innov_kernel(obs_rows, regions, blocks, metas, metas_1, metas_2, weights, pool, pool_2, scaled, proj):
    down = lax.broadcasted_iota(jnp.int32, (blocks, META_LANES), 0).astype(F32)
    mine = metas[META_ROWS * SELF + BLOCK_ROW : META_ROWS * SELF + BLOCK_ROW + 1, :]
    hot = jnp.where(down == mine, 1.0, 0.0).T.astype(BF16)
    per = META_LANES // obs_rows
    sub = lax.broadcasted_iota(jnp.int32, (per, META_LANES), 0)
    which = lax.broadcasted_iota(jnp.int32, (per, META_LANES), 1) // obs_rows
    picked = []
    for n in range(CLASSES):
        source = (metas, metas_1, metas_2)[n % 3]
        base = META_ROWS * (n // 3) + INNOV_ROW
        rows = [
            jnp.where(sub == which, source[base + i : base + i + 1, :], 0.0)
            for i in range(blocks // per)
        ]
        picked.append(dot(hot[CAP * n : CAP * (n + 1)], jnp.concatenate(rows, axis=0).astype(BF16)))
    p = lax.broadcasted_iota(jnp.int32, (META_LANES, META_LANES), 0) % obs_rows
    q = lax.broadcasted_iota(jnp.int32, (META_LANES, META_LANES), 1) % obs_rows
    spread = jnp.where(p == q, 1.0, 0.0).astype(BF16)
    repeated = dot(jnp.concatenate(picked, axis=0).astype(BF16), spread)
    folded = fold(repeated, obs_rows)
    lanes = jnp.concatenate([folded[i : i + 1] for i in range(folded.shape[0])], axis=1)
    wd = weights[...] * lanes
    high = wd.astype(BF16)
    both = jnp.concatenate([high.astype(F32), wd - high.astype(F32)], axis=0).astype(BF16)
    scaled[...] = both
    size = pool.shape[0]
    part = dot(both[:, SELF * size : (SELF + 1) * size], pool[...])
    part = part + dot(both[:, SECOND * size : (SECOND + 1) * size], pool_2[...])
    proj[...] = part[:regions] + part[regions:]


def quarters(x):
    return x[:128, :128], x[:128, 128:], x[128:, :128], x[128:, 128:]


def add_diagonal(x, d, eye):
    q = quarters(x)
    top = jnp.concatenate([q[0] + d * eye, q[1]], axis=1)
    low = jnp.concatenate([q[2], q[3] + d * eye], axis=1)
    return jnp.concatenate([top, low], axis=0)


def trace(x, eye):
    q = quarters(x)
    both = (q[0] + q[3]) * eye
    return jnp.sum(jnp.sum(both, axis=0, keepdims=True), axis=1, keepdims=True)


def roots(grams, proj_rows, eye, ensemble, between):
    each = range(len(grams))
    base = ensemble - 1.0
    scale = [
        base
        + jnp.max(jnp.sum(jnp.abs(grams[i]), axis=0, keepdims=True), axis=1, keepdims=True)
        for i in each
    ]
    inverse = [1.0 / scale[i] for i in each]
    mean = [trace(grams[i], eye) * (1.0 / ensemble) for i in each]
    u = [
        add_diagonal(grams[i] * (-0.5 * inverse[i]), 0.5 * inverse[i] * mean[i], eye)
        for i in each
    ]
    c = [1.0 - (base + mean[i]) * inverse[i] for i in each]
    a = [1.0 + 0.5 * c[i] for i in each]
    g = u
    ub = [u[i].astype(BF16) for i in each]
    gb = ub
    for step in range(NS_ITERS - 1):
        u2 = [dot(ub[i], ub[i]) for i in each]
        w = [((1.5 + 1.5 * c[i]) * u[i] + u2[i]).astype(BF16) for i in each]
        u3 = [dot(ub[i], w[i]) for i in each]
        between()
        u = [(1.5 * c[i] + 0.75 * c[i] * c[i]) * u[i] + u3[i] for i in each]
        c = [(0.75 + 0.25 * c[i]) * c[i] * c[i] for i in each]
        ub = [u[i].astype(BF16) for i in each]
        ug = [dot(ub[i], gb[i]) for i in each]
        g = [(1.0 + 0.5 * c[i]) * g[i] + a[i] * u[i] + ug[i] for i in each]
        gb = [g[i].astype(BF16) for i in each]
        a = [a[i] * (1.0 + 0.5 * c[i]) for i in each]
    first = lax.broadcasted_iota(jnp.int32, (16, ensemble), 0) < 8

    def times(i, v):
        high = v.astype(BF16).astype(F32)
        stacked = jnp.where(first, high, v - high).astype(BF16)
        q = dot(stacked, gb[i])
        return a[i] * v + q[0:1] + q[8:9]

    half = [times(i, proj_rows[i]) for i in each]
    wbar = [times(i, half[i]) * inverse[i] for i in each]
    factor = [lax.sqrt(base * inverse[i]) for i in each]
    return [(factor[i], factor[i] * a[i] - 1.0, g[i]) for i in each], wbar


EXTRAS = 5


def packed_rows(regions):
    return regions * 256 + -(-EXTRAS * regions // 16) * 16


def pack(matrix, wbar, eye, upper):
    factor, diagonal, g = matrix
    q = quarters(g)
    left = factor * q[0] + diagonal * eye
    right = factor * q[1]
    corner = factor * q[3] + diagonal * eye
    merged = jnp.where(upper, left, corner)
    high = wbar.astype(BF16).astype(F32)
    low = wbar - high
    extra = [
        jnp.sum(corner * eye, axis=0, keepdims=True),
        high[:, :128],
        high[:, 128:],
        low[:, :128],
        low[:, 128:],
    ]
    return right.astype(BF16), merged.astype(BF16), extra


def mix_regions(first, count, gram, proj, packed, between):
    n = 256
    down = lax.broadcasted_iota(jnp.int32, (128, 128), 0)
    across = lax.broadcasted_iota(jnp.int32, (128, 128), 1)
    eye = jnp.where(down == across, 1.0, 0.0)
    some = range(first, first + count)
    matrices, weights = roots(
        [gram[r - first] for r in some], [proj[r : r + 1, :] for r in some], eye, n, between
    )
    extras = []
    for k, r in enumerate(some):
        right, merged, extra = pack(matrices[k], weights[k], eye, down <= across)
        packed[n * r : n * r + 128, :] = right
        packed[n * r + 128 : n * (r + 1), :] = merged
        extras.append(extra)
    return extras


def mix_kernel(together, pool, weights, gram_near, scaled, proj_near, packed, proj):
    regions = proj.shape[0]
    size = pool.shape[0]
    part = dot(scaled[:, FIRST * size : (FIRST + 1) * size], pool[...])
    proj[...] = proj_near[...] + part[:regions] + part[regions:]
    parts = [(pool[...], transposed(pool[...]), FIRST * size)]

    def gram(r):
        return gram_near[256 * r : 256 * (r + 1), :] + gram_of(r, weights, parts)

    extras = []
    ready = [gram(r) for r in range(together)]
    for first in range(0, regions, together):
        later = []
        rest = list(range(first + together, min(first + 2 * together, regions)))

        def between(rest=rest, later=later):
            if rest:
                later.append(gram(rest.pop(0)))

        extras += mix_regions(first, together, ready, proj, packed, between)
        ready = later + [gram(r) for r in rest]
    rows = packed.shape[0] - 256 * regions
    below = jnp.zeros((rows - EXTRAS * regions, 128), F32)
    stacked = [extras[r][k] for k in range(EXTRAS) for r in range(regions)] + [below]
    packed[256 * regions :, :] = jnp.concatenate(stacked, axis=0).astype(BF16)


def unpack(count, packed, full):
    n = 256
    down = lax.broadcasted_iota(jnp.int32, (128, 128), 0)
    across = lax.broadcasted_iota(jnp.int32, (128, 128), 1)
    upper = down <= across
    lower = down > across
    extra = packed[n * count :, :].astype(F32)
    below = jnp.zeros((128 - extra.shape[0], 128), F32)
    columns = jnp.concatenate([extra, below], axis=0).T.astype(BF16)

    def spread(k):
        both = (down == k) | (down == k + 2 * count)
        return dot(columns, jnp.where(both, 1.0, 0.0).astype(BF16))

    for k in range(count):
        right = packed[n * k : n * k + 128, :].astype(F32)
        merged = packed[n * k + 128 : n * (k + 1), :].astype(F32)
        turned = merged.T
        top = spread(count + k)
        low = spread(2 * count + k)
        diagonal = extra[k : k + 1]
        corner = jnp.where(lower, merged, jnp.where(down == across, diagonal, turned))
        full[n * k : n * k + 128, :128] = (jnp.where(upper, merged, turned) + top).astype(BF16)
        full[n * k : n * k + 128, 128:] = (right + top).astype(BF16)
        full[n * k + 128 : n * (k + 1), :128] = (right.T + low).astype(BF16)
        full[n * k + 128 : n * (k + 1), 128:] = (corner + low).astype(BF16)


def block_places(table, first_slot, state_rows):
    return [
        pl.multiple_of(table[BLOCK_ROW, first_slot + i].astype(jnp.int32) * state_rows, state_rows)
        for i in range(CAP)
    ]


def scale_members(members, table, first_slot, places, count, left, state_rows):
    n = members.shape[1]
    for i in range(CAP):
        x = members[pl.ds(places[i], state_rows), :]
        for k in range(count):
            t = jnp.full((16, 128), table[k, first_slot + i], F32).astype(BF16)
            for u in range(state_rows // 16):
                for v in range(n // 128):
                    left[
                        state_rows * i + 16 * u : state_rows * i + 16 * (u + 1),
                        n * k + 128 * v : n * k + 128 * (v + 1),
                    ] = x[16 * u : 16 * (u + 1), 128 * v : 128 * (v + 1)] * t


def add_products(left, full, places, acc, state_rows):
    product = dot(left[...], full[...])
    for i in range(CAP):
        acc[pl.ds(places[i], state_rows), :] += product[state_rows * i : state_rows * (i + 1), :]


def increment_kernel(slots, halves, next_slots, start, state_rows, count, *refs):
    refs = list(refs)
    members = refs.pop(0)
    before = None if start else refs.pop(0)
    items, ahead = len(slots), len(next_slots)
    tables, refs = refs[: items + ahead], refs[items + ahead :]
    packed, refs = refs[:items], refs[items:]
    acc, lefts, scratch = refs[0], refs[1 : 1 + ahead], refs[1 + ahead :]
    rows = packed_rows(count)
    acc[...] = members[...].astype(F32) if start else before[...]
    for k, slot in enumerate(slots):
        left, full = scratch[2 * (k % 2) : 2 * (k % 2) + 2]
        places = block_places(tables[k], slot, state_rows)
        unpack(count, packed[k].at[rows * halves[k] : rows * (halves[k] + 1), :], full)
        scale_members(members, tables[k], slot, places, count, left, state_rows)
        add_products(left, full, places, acc, state_rows)
    for k, slot in enumerate(next_slots):
        table = tables[items + k]
        places = block_places(table, slot, state_rows)
        scale_members(members, table, slot, places, count, lefts[k], state_rows)


def finish_kernel(slots, halves, state_rows, count, before, *refs):
    items = len(slots)
    tables, packed, lefts = refs[:items], refs[items : 2 * items], refs[2 * items : 3 * items]
    out, acc, *fulls = refs[3 * items :]
    rows = packed_rows(count)
    acc[...] = before[...]
    for k in range(items):
        unpack(count, packed[k].at[rows * halves[k] : rows * (halves[k] + 1), :], fulls[k])
        places = block_places(tables[k], slots[k], state_rows)
        add_products(lefts[k], fulls[k], places, acc, state_rows)
    out[...] = acc[...].astype(BF16)


def from_band(x, place):
    count = lax.axis_size("band")
    step = 1 if place == FIRST else -1
    pairs = [(i + step * (1 - 2 * (i % 2)), i) for i in range(count)]
    return lax.ppermute(x, "band", [(j, i) for j, i in pairs if 0 <= j < count])


def from_lon(x, place):
    count = lax.axis_size("lon")
    step = -1 if place == FIRST else 1
    return lax.ppermute(
        x, "lon", [((i + step * (1 - 2 * (i % 2))) % count, i) for i in range(count)]
    )


def local(members, obs_perts, innovations, lists, placement, obs_taper, state_taper):
    lon_count = lax.axis_size("lon")
    blocks, state_rows, n = members.shape
    obs_rows = obs_perts.shape[1]
    regions, list_len = lists.shape
    entries = regions * list_len

    obs = obs_perts.reshape(blocks * obs_rows, n)
    obs_1 = from_band(obs, FIRST)
    obs_2 = from_band(obs, SECOND)

    meta, entry_slot, obs = call(
        functools.partial(table_kernel, (lon_count, blocks)),
        (
            jax.ShapeDtypeStruct((META_ROWS, META_LANES), F32),
            jax.ShapeDtypeStruct((entries, 128), F32),
            jax.ShapeDtypeStruct(obs.shape, BF16),
        ),
        [HBM_SPEC] * 5,
        "tables",
        10**9,
        10**6,
        [
            pltpu.VMEM(lists.shape, jnp.int32),
            pltpu.VMEM((placement.shape[0] // 128, 128), jnp.int32),
            pltpu.VMEM(state_taper.shape, F32),
            pltpu.VMEM(innovations.shape, BF16),
            pltpu.SemaphoreType.DMA((5,)),
        ],
    )(lists, placement.reshape(-1, 128), state_taper, innovations, obs)
    meta_1 = from_lon(meta, FIRST)
    meta_2 = from_lon(meta, SECOND)

    weights = call(
        functools.partial(weight_kernel, regions, list_len),
        jax.ShapeDtypeStruct((regions, CLASSES * CAP * obs_rows), F32),
        [VMEM_SPEC] * 2,
        "weights",
        10**9,
        10**6,
    )(entry_slot, jnp.swapaxes(obs_taper, 1, 2))
    obs_2, obs_1, weights = lax.optimization_barrier((obs_2, obs_1, weights))
    size = BAND_SLOTS * obs_rows
    pool_shape = jax.ShapeDtypeStruct((size, n), BF16)
    to_1, to_2 = call(
        functools.partial(select_kernel, obs_rows),
        (pool_shape, pool_shape),
        [VMEM_SPEC] * 3 + [SMEM_SPEC] * 2,
        "select",
        10**8,
        4 * 10**6,
    )(obs, obs_1, obs_2, meta_1, meta_2)
    pool_1 = from_lon(to_1, FIRST)
    pool_2 = from_lon(to_2, SECOND)
    metas = jnp.concatenate([meta, meta_1, meta_2], axis=0)
    metas_1 = from_band(metas, FIRST)
    metas_2 = from_band(metas, SECOND)

    region_flops = 2 * n**3
    gram_near, pool = call(
        functools.partial(near_gram_kernel, obs_rows, regions),
        (jax.ShapeDtypeStruct((regions * n, n), F32), pool_shape),
        [VMEM_SPEC] * 4 + [SMEM_SPEC] + [VMEM_SPEC],
        "near_gram",
        regions * 12 * region_flops,
        5 * 10**6,
    )(obs, obs_1, obs_2, pool_2, meta, weights)
    metas_2, metas_1, pool = lax.optimization_barrier((metas_2, metas_1, pool))
    proj_shape = jax.ShapeDtypeStruct((regions, n), F32)
    scaled, proj_near = call(
        functools.partial(innov_kernel, obs_rows, regions, blocks),
        (jax.ShapeDtypeStruct((2 * regions, 3 * size), BF16), proj_shape),
        [VMEM_SPEC] * 6,
        "innov",
        10**8,
        2 * 10**6,
    )(metas, metas_1, metas_2, weights, pool, pool_2)
    mix = call(
        functools.partial(mix_kernel, 4),
        jax.ShapeDtypeStruct((packed_rows(regions), 128), BF16),
        [VMEM_SPEC] * 5,
        "mixing",
        regions * 18 * region_flops,
        4 * 10**6,
        [pltpu.VMEM(proj_shape.shape, F32)],
    )(pool_1, weights, gram_near, scaled, proj_near)

    stacked = (metas, metas_1, metas_2)

    def table(lon, band):
        return stacked[band][META_ROWS * lon : META_ROWS * (lon + 1)]

    def slots(lon, band):
        return CAP * (lon * 3 + band)

    flat = members.reshape(blocks * state_rows, n)
    acc_shape = jax.ShapeDtypeStruct((blocks * state_rows, n), F32)
    scratch = [
        pltpu.VMEM((CAP * state_rows, regions * n), BF16),
        pltpu.VMEM((regions * n, n), BF16),
    ] * 2

    left_shape = jax.ShapeDtypeStruct((CAP * state_rows, regions * n), BF16)

    def increments(acc, groups, ahead, name):
        start = acc is None
        kernel = functools.partial(
            increment_kernel,
            [slots(*g) for g in groups],
            [arrived[g][1] for g in groups],
            [slots(*g) for g in ahead],
            start,
            state_rows,
            regions,
        )
        return call(
            kernel,
            (acc_shape,) + (left_shape,) * len(ahead),
            [VMEM_SPEC] * (1 if start else 2)
            + [SMEM_SPEC] * (len(groups) + len(ahead))
            + [VMEM_SPEC] * len(groups),
            name,
            len(groups) * 3 * regions * region_flops,
            6 * 10**6,
            scratch,
        )(
            *([flat] if start else [flat, acc]),
            *[table(*g) for g in groups + ahead],
            *[arrived[g][0] for g in groups],
        )

    arrived = {(SELF, SELF): (mix, 0)}
    for lon in (SECOND, FIRST):
        arrived[lon, SELF] = (from_lon(mix, lon), 0)
    mix_2 = from_band(mix, SECOND)
    mix_1 = from_band(mix, FIRST)
    (acc,) = increments(None, [(SELF, SELF), (SECOND, SELF)], [], "own")
    near, mix_2, mix_1, acc = lax.optimization_barrier(
        (arrived[FIRST, SELF][0], mix_2, mix_1, acc)
    )
    arrived[FIRST, SELF] = (near, 0)
    both = jnp.concatenate([mix_1, mix_2], axis=0)
    arrived[SELF, FIRST], arrived[SELF, SECOND] = (mix_1, 0), (mix_2, 0)
    for lon in (FIRST, SECOND):
        there = from_lon(both, lon)
        arrived[lon, FIRST], arrived[lon, SECOND] = (there, 0), (there, 1)
    last = [(FIRST, FIRST), (FIRST, SECOND)]
    (acc,) = increments(acc, [(SELF, FIRST), (SELF, SECOND), (FIRST, SELF)], [], "inner")
    acc, *lefts = increments(acc, [(SECOND, FIRST), (SECOND, SECOND)], last, "outer")
    out = call(
        functools.partial(
            finish_kernel,
            [slots(*g) for g in last],
            [arrived[g][1] for g in last],
            state_rows,
            regions,
        ),
        jax.ShapeDtypeStruct(acc_shape.shape, BF16),
        [VMEM_SPEC] + [SMEM_SPEC] * 2 + [VMEM_SPEC] * 4,
        "finish",
        6 * regions * region_flops,
        9 * 10**6,
        [pltpu.VMEM(acc_shape.shape, F32)] + [pltpu.VMEM((regions * n, n), BF16)] * 2,
    )(acc, *[table(*g) for g in last], *[arrived[g][0] for g in last], *lefts)
    return out.reshape(members.shape)


def solution(mesh):
    in_specs = (
        P(("band", "lon"), None, None),
        P(("band", "lon"), None, None),
        P(("band", "lon"), None),
        P(("band", "lon"), None),
        P(),
        P(("band", "lon"), None, None),
        P(("band", "lon"), None),
    )
    out_specs = P(("band", "lon"), None, None)
    return jax.shard_map(local, mesh=mesh, in_specs=in_specs, out_specs=out_specs, check_vma=False)
```

```python
import functools

import jax
import jax.numpy as jnp
from jax import lax
from jax.experimental import pallas as pl
from jax.experimental.pallas import tpu as pltpu
from jax.sharding import PartitionSpec as P

NS_ITERS = 5
CAP = 16
SELF, FIRST, SECOND = 0, 1, 2
CLASSES = 9
BAND_SLOTS = 3 * CAP
CLASS_STRIDE = 64
KEYS = 640
META_LANES = 256
META_ROWS = 16
BLOCK_ROW = 8
INNOV_ROW = 9

F32 = jnp.float32
BF16 = jnp.bfloat16
VMEM_SPEC = pl.BlockSpec(memory_space=pltpu.VMEM)
SMEM_SPEC = pl.BlockSpec(memory_space=pltpu.SMEM)
HBM_SPEC = pl.BlockSpec(memory_space=pltpu.HBM)


def dot(a, b):
    return jnp.dot(a, b, preferred_element_type=F32)


def call(kernel, outs, in_specs, name, flops, bytes_accessed, scratch=(), aliases=None):
    return pl.pallas_call(
        kernel,
        out_shape=outs,
        in_specs=in_specs,
        out_specs=jax.tree.map(lambda _: VMEM_SPEC, outs),
        scratch_shapes=list(scratch),
        input_output_aliases=aliases or {},
        compiler_params=pltpu.CompilerParams(vmem_limit_bytes=40 * 1024 * 1024),
        cost_estimate=pl.CostEstimate(
            flops=flops, bytes_accessed=bytes_accessed, transcendentals=0
        ),
        name=name,
    )


def fold(x, width):
    per = META_LANES // width
    sub = lax.broadcasted_iota(jnp.int32, (per, META_LANES), 0)
    which = lax.broadcasted_iota(jnp.int32, (per, META_LANES), 1) // width
    return jnp.concatenate(
        [
            jnp.sum(jnp.where(sub == which, x[i : i + per], 0.0), axis=0, keepdims=True)
            for i in range(0, x.shape[0], per)
        ],
        axis=0,
    )


def table_kernel(shape, *refs):
    lon_count, blocks = shape
    sources, (meta, entry_slot, obs), copies, sems = refs[:5], refs[5:8], refs[8:12], refs[12]
    transfers = [
        pltpu.make_async_copy(source, to, sems.at[k])
        for k, (source, to) in enumerate(zip(sources, copies + (obs,)))
    ]
    for transfer in transfers:
        transfer.start()
    for transfer in transfers[:-1]:
        transfer.wait()
    lists, placement, state, innov = copies
    regions, list_len = lists.shape
    entries = regions * list_len
    obs_rows = innov.shape[1]
    p = lax.broadcasted_iota(jnp.int32, (obs_rows, META_LANES), 0)
    q = lax.broadcasted_iota(jnp.int32, (obs_rows, META_LANES), 1) % obs_rows
    repeated = dot(innov[...], jnp.where(p == q, 1.0, 0.0).astype(BF16))
    meta[...] = jnp.zeros_like(meta)
    folded = fold(repeated, obs_rows)
    meta[INNOV_ROW : INNOV_ROW + folded.shape[0], :] = folded

    def columns(x):
        t = x.T
        return jnp.concatenate(
            [jnp.broadcast_to(t[:, r : r + 1], (list_len, 128)) for r in range(regions)], axis=0
        )

    lane = lax.broadcasted_iota(jnp.int32, (1, 128), 1).astype(F32)
    ones = jnp.ones((128, 128), BF16)
    ids = columns(lists[...].astype(F32))
    line = jnp.floor(ids * (1.0 / 128.0))
    table_rows = placement.shape[0]
    line_hot = jnp.where(line == lane, 1.0, 0.0).astype(BF16)[:, :table_rows]
    at = lane == ids - 128.0 * line
    places = placement[...].astype(F32)
    high = jnp.floor(places * (1.0 / 64.0))

    def look(part):
        found = dot(line_hot, part.astype(BF16))
        return dot(jnp.where(at, found, 0.0).astype(BF16), ones)

    row = 64.0 * look(high) + look(places - 64.0 * high)
    holder = jnp.floor((row + 0.5) * (1.0 / blocks))
    inside = row - blocks * holder
    holder_band = jnp.floor((holder + 0.5) * (1.0 / lon_count))
    band_here = lax.axis_index("band")
    lon_here = lax.axis_index("lon")
    band_step = holder_band - band_here.astype(F32)
    lon_step = holder - lon_count * holder_band - lon_here.astype(F32)
    half = lon_count // 2
    lon_step = jnp.where(lon_step < -half, lon_step + lon_count, lon_step)
    lon_step = jnp.where(lon_step > half, lon_step - lon_count, lon_step)
    band_turn = band_step * (1 - 2 * (band_here % 2)).astype(F32)
    lon_turn = lon_step * (2 * (lon_here % 2) - 1).astype(F32)
    band_place = jnp.where(band_turn == 0.0, 0.0, jnp.where(band_turn > 0.0, 1.0, 2.0))
    lon_place = jnp.where(lon_turn == 0.0, 0.0, jnp.where(lon_turn > 0.0, 1.0, 2.0))
    key = (lon_place * 3.0 + band_place) * CLASS_STRIDE + inside

    hot = jnp.concatenate(
        [jnp.where(key == lane + 128.0 * c, 1.0, 0.0) for c in range(KEYS // 128)], axis=1
    ).astype(BF16)
    counts = lax.dot_general(
        hot,
        jnp.ones((entries, 128), BF16),
        (((0,), (0,)), ((), ())),
        preferred_element_type=F32,
    )
    present = jnp.minimum(counts, 1.0)
    down = lax.broadcasted_iota(jnp.int32, (KEYS, KEYS), 0)
    across = lax.broadcasted_iota(jnp.int32, (KEYS, KEYS), 1)
    before = (across < down) & (across // CLASS_STRIDE == down // CLASS_STRIDE)
    rank = dot(jnp.where(before, 1.0, 0.0).astype(BF16), present.astype(BF16))
    key_id = lax.broadcasted_iota(jnp.int32, (KEYS, 128), 0)
    slot = rank + (CAP * (key_id // CLASS_STRIDE)).astype(F32)
    block = (key_id % CLASS_STRIDE).astype(F32)
    slots = dot(hot, slot.astype(BF16))
    entry_slot[...] = slots
    tapers = columns(state[...])
    for c in range(2):
        match = (slot == lane + 128.0 * c) & (present > 0.0)
        rows = jnp.sum(jnp.where(match, block, 0.0), axis=0, keepdims=True)
        meta[BLOCK_ROW : BLOCK_ROW + 1, 128 * c : 128 * (c + 1)] = rows
        hit = jnp.where(slots == lane + 128.0 * c, tapers, 0.0)
        for r in range(regions):
            meta[r : r + 1, 128 * c : 128 * (c + 1)] = jnp.sum(
                hit[r * list_len : (r + 1) * list_len], axis=0, keepdims=True
            )
    transfers[-1].wait()


def weight_kernel(regions, list_len, entry_slot, taper, weights):
    obs_rows = taper.shape[1]
    group = (lax.broadcasted_iota(jnp.int32, (1, 128), 1) // obs_rows).astype(F32)
    p = lax.broadcasted_iota(jnp.int32, (obs_rows, 128), 0)
    q = lax.broadcasted_iota(jnp.int32, (obs_rows, 128), 1) % obs_rows
    spread = jnp.where(p == q, 1.0, 0.0).astype(BF16)

    def across(x):
        return lax.dot_general(
            x, spread, (((0,), (0,)), ((), ())), preferred_element_type=F32
        )

    for r in range(regions):
        mine = entry_slot[r * list_len : (r + 1) * list_len, :]
        high = taper[r].astype(BF16)
        low = (taper[r] - high.astype(F32)).astype(BF16)
        w = across(high) + across(low)
        for c in range(CLASSES * CAP // 4):
            hit = mine == group + 4.0 * c
            weights[r : r + 1, 128 * c : 128 * (c + 1)] = jnp.sum(
                jnp.where(hit, w, 0.0), axis=0, keepdims=True
            )


def gather_blocks(sources, table, first_slot, obs_rows, out):
    for k, source in enumerate(sources):
        for i in range(CAP):
            block = table[BLOCK_ROW, first_slot + CAP * k + i].astype(jnp.int32)
            at = pl.multiple_of(block * obs_rows, obs_rows)
            to = (CAP * k + i) * obs_rows
            out[to : to + obs_rows, :] = source[pl.ds(at, obs_rows), :]


def select_kernel(obs_rows, obs, obs_1, obs_2, table_1, table_2, to_1, to_2):
    sources = (obs, obs_1, obs_2)
    gather_blocks(sources, table_1, FIRST * BAND_SLOTS, obs_rows, to_1)
    gather_blocks(sources, table_2, SECOND * BAND_SLOTS, obs_rows, to_2)


def transposed(y):
    return jnp.concatenate(
        [y[256 * c : 256 * (c + 1)].astype(F32).T.astype(BF16) for c in range(y.shape[0] // 256)],
        axis=1,
    )


def near_gram_kernel(obs_rows, regions, obs, obs_1, obs_2, pool_2, table, weights, gram, pool):
    gather_blocks((obs, obs_1, obs_2), table, SELF * BAND_SLOTS, obs_rows, pool)
    size = pool.shape[0]
    parts = [(y[...], transposed(y[...]), at * size) for y, at in ((pool, SELF), (pool_2, SECOND))]
    for r in range(regions):
        gram[256 * r : 256 * (r + 1), :] = gram_of(r, weights, parts)


def gram_of(r, weights, parts):
    products = [
        dot(y_t * weights[r : r + 1, lane : lane + y.shape[0]].astype(BF16), y)
        for y, y_t, lane in parts
    ]
    return sum(products[1:], products[0])


def innov_kernel(obs_rows, regions, blocks, metas, metas_1, metas_2, weights, pool, pool_2, scaled, proj):
    down = lax.broadcasted_iota(jnp.int32, (blocks, META_LANES), 0).astype(F32)
    mine = metas[META_ROWS * SELF + BLOCK_ROW : META_ROWS * SELF + BLOCK_ROW + 1, :]
    hot = jnp.where(down == mine, 1.0, 0.0).T.astype(BF16)
    per = META_LANES // obs_rows
    sub = lax.broadcasted_iota(jnp.int32, (per, META_LANES), 0)
    which = lax.broadcasted_iota(jnp.int32, (per, META_LANES), 1) // obs_rows
    picked = []
    for n in range(CLASSES):
        source = (metas, metas_1, metas_2)[n % 3]
        base = META_ROWS * (n // 3) + INNOV_ROW
        rows = [
            jnp.where(sub == which, source[base + i : base + i + 1, :], 0.0)
            for i in range(blocks // per)
        ]
        picked.append(dot(hot[CAP * n : CAP * (n + 1)], jnp.concatenate(rows, axis=0).astype(BF16)))
    p = lax.broadcasted_iota(jnp.int32, (META_LANES, META_LANES), 0) % obs_rows
    q = lax.broadcasted_iota(jnp.int32, (META_LANES, META_LANES), 1) % obs_rows
    spread = jnp.where(p == q, 1.0, 0.0).astype(BF16)
    repeated = dot(jnp.concatenate(picked, axis=0).astype(BF16), spread)
    folded = fold(repeated, obs_rows)
    lanes = jnp.concatenate([folded[i : i + 1] for i in range(folded.shape[0])], axis=1)
    wd = weights[...] * lanes
    high = wd.astype(BF16)
    both = jnp.concatenate([high.astype(F32), wd - high.astype(F32)], axis=0).astype(BF16)
    scaled[...] = both
    size = pool.shape[0]
    part = dot(both[:, SELF * size : (SELF + 1) * size], pool[...])
    part = part + dot(both[:, SECOND * size : (SECOND + 1) * size], pool_2[...])
    proj[...] = part[:regions] + part[regions:]


def quarters(x):
    return x[:128, :128], x[:128, 128:], x[128:, :128], x[128:, 128:]


def add_diagonal(x, d, eye):
    q = quarters(x)
    top = jnp.concatenate([q[0] + d * eye, q[1]], axis=1)
    low = jnp.concatenate([q[2], q[3] + d * eye], axis=1)
    return jnp.concatenate([top, low], axis=0)


def trace(x, eye):
    q = quarters(x)
    both = (q[0] + q[3]) * eye
    return jnp.sum(jnp.sum(both, axis=0, keepdims=True), axis=1, keepdims=True)


def roots(grams, proj_rows, eye, ensemble, between):
    each = range(len(grams))
    base = ensemble - 1.0
    scale = [
        base
        + jnp.max(jnp.sum(jnp.abs(grams[i]), axis=0, keepdims=True), axis=1, keepdims=True)
        for i in each
    ]
    inverse = [1.0 / scale[i] for i in each]
    mean = [trace(grams[i], eye) * (1.0 / ensemble) for i in each]
    u = [
        add_diagonal(grams[i] * (-0.5 * inverse[i]), 0.5 * inverse[i] * mean[i], eye)
        for i in each
    ]
    c = [1.0 - (base + mean[i]) * inverse[i] for i in each]
    a = [1.0 + 0.5 * c[i] for i in each]
    g = u
    ub = [u[i].astype(BF16) for i in each]
    gb = ub
    for step in range(NS_ITERS - 1):
        u2 = [dot(ub[i], ub[i]) for i in each]
        w = [((1.5 + 1.5 * c[i]) * u[i] + u2[i]).astype(BF16) for i in each]
        u3 = [dot(ub[i], w[i]) for i in each]
        between()
        u = [(1.5 * c[i] + 0.75 * c[i] * c[i]) * u[i] + u3[i] for i in each]
        c = [(0.75 + 0.25 * c[i]) * c[i] * c[i] for i in each]
        ub = [u[i].astype(BF16) for i in each]
        ug = [dot(ub[i], gb[i]) for i in each]
        g = [(1.0 + 0.5 * c[i]) * g[i] + a[i] * u[i] + ug[i] for i in each]
        gb = [g[i].astype(BF16) for i in each]
        a = [a[i] * (1.0 + 0.5 * c[i]) for i in each]
    first = lax.broadcasted_iota(jnp.int32, (16, ensemble), 0) < 8

    def times(i, v):
        high = v.astype(BF16).astype(F32)
        stacked = jnp.where(first, high, v - high).astype(BF16)
        q = dot(stacked, gb[i])
        return a[i] * v + q[0:1] + q[8:9]

    half = [times(i, proj_rows[i]) for i in each]
    wbar = [times(i, half[i]) * inverse[i] for i in each]
    factor = [lax.sqrt(base * inverse[i]) for i in each]
    return [(factor[i], factor[i] * a[i] - 1.0, g[i]) for i in each], wbar


EXTRAS = 5


def packed_rows(regions):
    return regions * 256 + -(-EXTRAS * regions // 16) * 16


def pack(matrix, wbar, eye, upper):
    factor, diagonal, g = matrix
    q = quarters(g)
    left = factor * q[0] + diagonal * eye
    right = factor * q[1]
    corner = factor * q[3] + diagonal * eye
    merged = jnp.where(upper, left, corner)
    high = wbar.astype(BF16).astype(F32)
    low = wbar - high
    extra = [
        jnp.sum(corner * eye, axis=0, keepdims=True),
        high[:, :128],
        high[:, 128:],
        low[:, :128],
        low[:, 128:],
    ]
    return right.astype(BF16), merged.astype(BF16), extra


def mix_regions(first, count, gram, proj, packed, between):
    n = 256
    down = lax.broadcasted_iota(jnp.int32, (128, 128), 0)
    across = lax.broadcasted_iota(jnp.int32, (128, 128), 1)
    eye = jnp.where(down == across, 1.0, 0.0)
    some = range(first, first + count)
    matrices, weights = roots(
        [gram[r - first] for r in some], [proj[r : r + 1, :] for r in some], eye, n, between
    )
    extras = []
    for k, r in enumerate(some):
        right, merged, extra = pack(matrices[k], weights[k], eye, down <= across)
        packed[n * r : n * r + 128, :] = right
        packed[n * r + 128 : n * (r + 1), :] = merged
        extras.append(extra)
    return extras


def mix_kernel(together, pool, weights, gram_near, scaled, proj_near, packed, proj):
    regions = proj.shape[0]
    size = pool.shape[0]
    part = dot(scaled[:, FIRST * size : (FIRST + 1) * size], pool[...])
    proj[...] = proj_near[...] + part[:regions] + part[regions:]
    parts = [(pool[...], transposed(pool[...]), FIRST * size)]

    def gram(r):
        return gram_near[256 * r : 256 * (r + 1), :] + gram_of(r, weights, parts)

    extras = []
    ready = [gram(r) for r in range(together)]
    for first in range(0, regions, together):
        later = []
        rest = list(range(first + together, min(first + 2 * together, regions)))

        def between(rest=rest, later=later):
            if rest:
                later.append(gram(rest.pop(0)))

        extras += mix_regions(first, together, ready, proj, packed, between)
        ready = later + [gram(r) for r in rest]
    rows = packed.shape[0] - 256 * regions
    below = jnp.zeros((rows - EXTRAS * regions, 128), F32)
    stacked = [extras[r][k] for k in range(EXTRAS) for r in range(regions)] + [below]
    packed[256 * regions :, :] = jnp.concatenate(stacked, axis=0).astype(BF16)


def unpack(count, packed, full):
    n = 256
    down = lax.broadcasted_iota(jnp.int32, (128, 128), 0)
    across = lax.broadcasted_iota(jnp.int32, (128, 128), 1)
    upper = down <= across
    lower = down > across
    extra = packed[n * count :, :].astype(F32)
    below = jnp.zeros((128 - extra.shape[0], 128), F32)
    columns = jnp.concatenate([extra, below], axis=0).T.astype(BF16)

    def spread(k):
        both = (down == k) | (down == k + 2 * count)
        return dot(columns, jnp.where(both, 1.0, 0.0).astype(BF16))

    for k in range(count):
        right = packed[n * k : n * k + 128, :].astype(F32)
        merged = packed[n * k + 128 : n * (k + 1), :].astype(F32)
        turned = merged.T
        top = spread(count + k)
        low = spread(2 * count + k)
        diagonal = extra[k : k + 1]
        corner = jnp.where(lower, merged, jnp.where(down == across, diagonal, turned))
        full[n * k : n * k + 128, :128] = (jnp.where(upper, merged, turned) + top).astype(BF16)
        full[n * k : n * k + 128, 128:] = (right + top).astype(BF16)
        full[n * k + 128 : n * (k + 1), :128] = (right.T + low).astype(BF16)
        full[n * k + 128 : n * (k + 1), 128:] = (corner + low).astype(BF16)


def block_places(table, first_slot, state_rows):
    return [
        pl.multiple_of(table[BLOCK_ROW, first_slot + i].astype(jnp.int32) * state_rows, state_rows)
        for i in range(CAP)
    ]


def scale_members(members, table, first_slot, places, count, left, state_rows):
    n = members.shape[1]
    for i in range(CAP):
        x = members[pl.ds(places[i], state_rows), :]
        for k in range(count):
            t = jnp.full((16, 128), table[k, first_slot + i], F32).astype(BF16)
            for u in range(state_rows // 16):
                for v in range(n // 128):
                    left[
                        state_rows * i + 16 * u : state_rows * i + 16 * (u + 1),
                        n * k + 128 * v : n * k + 128 * (v + 1),
                    ] = x[16 * u : 16 * (u + 1), 128 * v : 128 * (v + 1)] * t


def add_products(left, full, places, acc, state_rows):
    product = dot(left[...], full[...])
    for i in range(CAP):
        acc[pl.ds(places[i], state_rows), :] += product[state_rows * i : state_rows * (i + 1), :]


def increment_kernel(slots, halves, next_slots, start, state_rows, count, *refs):
    refs = list(refs)
    members = refs.pop(0)
    before = None if start else refs.pop(0)
    items, ahead = len(slots), len(next_slots)
    tables, refs = refs[: items + ahead], refs[items + ahead :]
    packed, refs = refs[:items], refs[items:]
    acc, lefts, scratch = refs[0], refs[1 : 1 + ahead], refs[1 + ahead :]
    rows = packed_rows(count)
    acc[...] = members[...].astype(F32) if start else before[...]
    for k, slot in enumerate(slots):
        left, full = scratch[2 * (k % 2) : 2 * (k % 2) + 2]
        places = block_places(tables[k], slot, state_rows)
        unpack(count, packed[k].at[rows * halves[k] : rows * (halves[k] + 1), :], full)
        scale_members(members, tables[k], slot, places, count, left, state_rows)
        add_products(left, full, places, acc, state_rows)
    for k, slot in enumerate(next_slots):
        table = tables[items + k]
        places = block_places(table, slot, state_rows)
        scale_members(members, table, slot, places, count, lefts[k], state_rows)


def finish_kernel(slots, halves, state_rows, count, before, *refs):
    items = len(slots)
    tables, packed, lefts = refs[:items], refs[items : 2 * items], refs[2 * items : 3 * items]
    out, acc, *fulls = refs[3 * items :]
    rows = packed_rows(count)
    acc[...] = before[...]
    for k in range(items):
        unpack(count, packed[k].at[rows * halves[k] : rows * (halves[k] + 1), :], fulls[k])
        places = block_places(tables[k], slots[k], state_rows)
        add_products(lefts[k], fulls[k], places, acc, state_rows)
    out[...] = acc[...].astype(BF16)


def from_band(x, place):
    count = lax.axis_size("band")
    step = 1 if place == FIRST else -1
    pairs = [(i + step * (1 - 2 * (i % 2)), i) for i in range(count)]
    return lax.ppermute(x, "band", [(j, i) for j, i in pairs if 0 <= j < count])


def from_lon(x, place):
    count = lax.axis_size("lon")
    step = -1 if place == FIRST else 1
    return lax.ppermute(
        x, "lon", [((i + step * (1 - 2 * (i % 2))) % count, i) for i in range(count)]
    )


def local(members, obs_perts, innovations, lists, placement, obs_taper, state_taper):
    lon_count = lax.axis_size("lon")
    blocks, state_rows, n = members.shape
    obs_rows = obs_perts.shape[1]
    regions, list_len = lists.shape
    entries = regions * list_len

    obs = obs_perts.reshape(blocks * obs_rows, n)
    obs_1 = from_band(obs, FIRST)
    obs_2 = from_band(obs, SECOND)

    meta, entry_slot, obs = call(
        functools.partial(table_kernel, (lon_count, blocks)),
        (
            jax.ShapeDtypeStruct((META_ROWS, META_LANES), F32),
            jax.ShapeDtypeStruct((entries, 128), F32),
            jax.ShapeDtypeStruct(obs.shape, BF16),
        ),
        [HBM_SPEC] * 5,
        "tables",
        10**9,
        10**6,
        [
            pltpu.VMEM(lists.shape, jnp.int32),
            pltpu.VMEM((placement.shape[0] // 128, 128), jnp.int32),
            pltpu.VMEM(state_taper.shape, F32),
            pltpu.VMEM(innovations.shape, BF16),
            pltpu.SemaphoreType.DMA((5,)),
        ],
    )(lists, placement.reshape(-1, 128), state_taper, innovations, obs)
    meta_1 = from_lon(meta, FIRST)
    meta_2 = from_lon(meta, SECOND)

    weights = call(
        functools.partial(weight_kernel, regions, list_len),
        jax.ShapeDtypeStruct((regions, CLASSES * CAP * obs_rows), F32),
        [VMEM_SPEC] * 2,
        "weights",
        10**9,
        10**6,
    )(entry_slot, jnp.swapaxes(obs_taper, 1, 2))
    obs_2, obs_1, weights = lax.optimization_barrier((obs_2, obs_1, weights))
    size = BAND_SLOTS * obs_rows
    pool_shape = jax.ShapeDtypeStruct((size, n), BF16)
    to_1, to_2 = call(
        functools.partial(select_kernel, obs_rows),
        (pool_shape, pool_shape),
        [VMEM_SPEC] * 3 + [SMEM_SPEC] * 2,
        "select",
        10**8,
        4 * 10**6,
    )(obs, obs_1, obs_2, meta_1, meta_2)
    pool_1 = from_lon(to_1, FIRST)
    pool_2 = from_lon(to_2, SECOND)
    metas = jnp.concatenate([meta, meta_1, meta_2], axis=0)
    metas_1 = from_band(metas, FIRST)
    metas_2 = from_band(metas, SECOND)

    region_flops = 2 * n**3
    gram_near, pool = call(
        functools.partial(near_gram_kernel, obs_rows, regions),
        (jax.ShapeDtypeStruct((regions * n, n), F32), pool_shape),
        [VMEM_SPEC] * 4 + [SMEM_SPEC] + [VMEM_SPEC],
        "near_gram",
        regions * 12 * region_flops,
        5 * 10**6,
    )(obs, obs_1, obs_2, pool_2, meta, weights)
    metas_2, metas_1, pool = lax.optimization_barrier((metas_2, metas_1, pool))
    proj_shape = jax.ShapeDtypeStruct((regions, n), F32)
    scaled, proj_near = call(
        functools.partial(innov_kernel, obs_rows, regions, blocks),
        (jax.ShapeDtypeStruct((2 * regions, 3 * size), BF16), proj_shape),
        [VMEM_SPEC] * 6,
        "innov",
        10**8,
        2 * 10**6,
    )(metas, metas_1, metas_2, weights, pool, pool_2)
    mix = call(
        functools.partial(mix_kernel, 4),
        jax.ShapeDtypeStruct((packed_rows(regions), 128), BF16),
        [VMEM_SPEC] * 5,
        "mixing",
        regions * 18 * region_flops,
        4 * 10**6,
        [pltpu.VMEM(proj_shape.shape, F32)],
    )(pool_1, weights, gram_near, scaled, proj_near)

    stacked = (metas, metas_1, metas_2)

    def table(lon, band):
        return stacked[band][META_ROWS * lon : META_ROWS * (lon + 1)]

    def slots(lon, band):
        return CAP * (lon * 3 + band)

    flat = members.reshape(blocks * state_rows, n)
    acc_shape = jax.ShapeDtypeStruct((blocks * state_rows, n), F32)
    scratch = [
        pltpu.VMEM((CAP * state_rows, regions * n), BF16),
        pltpu.VMEM((regions * n, n), BF16),
    ] * 2

    left_shape = jax.ShapeDtypeStruct((CAP * state_rows, regions * n), BF16)

    def increments(acc, groups, ahead, name):
        start = acc is None
        kernel = functools.partial(
            increment_kernel,
            [slots(*g) for g in groups],
            [arrived[g][1] for g in groups],
            [slots(*g) for g in ahead],
            start,
            state_rows,
            regions,
        )
        return call(
            kernel,
            (acc_shape,) + (left_shape,) * len(ahead),
            [VMEM_SPEC] * (1 if start else 2)
            + [SMEM_SPEC] * (len(groups) + len(ahead))
            + [VMEM_SPEC] * len(groups),
            name,
            len(groups) * 3 * regions * region_flops,
            6 * 10**6,
            scratch,
        )(
            *([flat] if start else [flat, acc]),
            *[table(*g) for g in groups + ahead],
            *[arrived[g][0] for g in groups],
        )

    arrived = {(SELF, SELF): (mix, 0)}
    for lon in (SECOND, FIRST):
        arrived[lon, SELF] = (from_lon(mix, lon), 0)
    mix_2 = from_band(mix, SECOND)
    mix_1 = from_band(mix, FIRST)
    (acc,) = increments(None, [(SELF, SELF), (SECOND, SELF)], [], "own")
    near, mix_2, mix_1, acc = lax.optimization_barrier(
        (arrived[FIRST, SELF][0], mix_2, mix_1, acc)
    )
    arrived[FIRST, SELF] = (near, 0)
    arrived[FIRST, FIRST] = (from_band(near, FIRST), 0)
    arrived[FIRST, SECOND] = (from_band(near, SECOND), 0)
    arrived[SELF, FIRST], arrived[SELF, SECOND] = (mix_1, 0), (mix_2, 0)
    both = from_lon(jnp.concatenate([mix_1, mix_2], axis=0), SECOND)
    arrived[SECOND, FIRST], arrived[SECOND, SECOND] = (both, 0), (both, 1)
    last = [(FIRST, FIRST), (FIRST, SECOND)]
    (acc,) = increments(acc, [(SELF, FIRST), (SELF, SECOND), (FIRST, SELF)], [], "inner")
    acc, *lefts = increments(acc, [(SECOND, FIRST), (SECOND, SECOND)], last, "outer")
    out = call(
        functools.partial(
            finish_kernel,
            [slots(*g) for g in last],
            [arrived[g][1] for g in last],
            state_rows,
            regions,
        ),
        jax.ShapeDtypeStruct(acc_shape.shape, BF16),
        [VMEM_SPEC] + [SMEM_SPEC] * 2 + [VMEM_SPEC] * 4,
        "finish",
        6 * regions * region_flops,
        9 * 10**6,
        [pltpu.VMEM(acc_shape.shape, F32)] + [pltpu.VMEM((regions * n, n), BF16)] * 2,
    )(acc, *[table(*g) for g in last], *[arrived[g][0] for g in last], *lefts)
    return out.reshape(members.shape)


def solution(mesh):
    in_specs = (
        P(("band", "lon"), None, None),
        P(("band", "lon"), None, None),
        P(("band", "lon"), None),
        P(("band", "lon"), None),
        P(),
        P(("band", "lon"), None, None),
        P(("band", "lon"), None),
    )
    out_specs = P(("band", "lon"), None, None)
    return jax.shard_map(local, mesh=mesh, in_specs=in_specs, out_specs=out_specs, check_vma=False)
```

```python
import functools

import jax
import jax.numpy as jnp
from jax import lax
from jax.experimental import pallas as pl
from jax.experimental.pallas import tpu as pltpu
from jax.sharding import PartitionSpec as P

NS_ITERS = 5
CAP = 16
SELF, FIRST, SECOND = 0, 1, 2
CLASSES = 9
BAND_SLOTS = 3 * CAP
CLASS_STRIDE = 64
KEYS = 640
META_LANES = 256
META_ROWS = 16
BLOCK_ROW = 8
INNOV_ROW = 9

F32 = jnp.float32
BF16 = jnp.bfloat16
VMEM_SPEC = pl.BlockSpec(memory_space=pltpu.VMEM)
SMEM_SPEC = pl.BlockSpec(memory_space=pltpu.SMEM)
HBM_SPEC = pl.BlockSpec(memory_space=pltpu.HBM)


def dot(a, b):
    return jnp.dot(a, b, preferred_element_type=F32)


def call(kernel, outs, in_specs, name, flops, bytes_accessed, scratch=(), aliases=None):
    return pl.pallas_call(
        kernel,
        out_shape=outs,
        in_specs=in_specs,
        out_specs=jax.tree.map(lambda _: VMEM_SPEC, outs),
        scratch_shapes=list(scratch),
        input_output_aliases=aliases or {},
        compiler_params=pltpu.CompilerParams(vmem_limit_bytes=40 * 1024 * 1024),
        cost_estimate=pl.CostEstimate(
            flops=flops, bytes_accessed=bytes_accessed, transcendentals=0
        ),
        name=name,
    )


def fold(x, width):
    per = META_LANES // width
    sub = lax.broadcasted_iota(jnp.int32, (per, META_LANES), 0)
    which = lax.broadcasted_iota(jnp.int32, (per, META_LANES), 1) // width
    return jnp.concatenate(
        [
            jnp.sum(jnp.where(sub == which, x[i : i + per], 0.0), axis=0, keepdims=True)
            for i in range(0, x.shape[0], per)
        ],
        axis=0,
    )


def table_kernel(shape, *refs):
    lon_count, blocks = shape
    sources, (meta, entry_slot, obs), copies, sems = refs[:5], refs[5:8], refs[8:12], refs[12]
    transfers = [
        pltpu.make_async_copy(source, to, sems.at[k])
        for k, (source, to) in enumerate(zip(sources, copies + (obs,)))
    ]
    for transfer in transfers:
        transfer.start()
    for transfer in transfers[:-1]:
        transfer.wait()
    lists, placement, state, innov = copies
    regions, list_len = lists.shape
    entries = regions * list_len
    obs_rows = innov.shape[1]
    p = lax.broadcasted_iota(jnp.int32, (obs_rows, META_LANES), 0)
    q = lax.broadcasted_iota(jnp.int32, (obs_rows, META_LANES), 1) % obs_rows
    repeated = dot(innov[...], jnp.where(p == q, 1.0, 0.0).astype(BF16))
    meta[...] = jnp.zeros_like(meta)
    folded = fold(repeated, obs_rows)
    meta[INNOV_ROW : INNOV_ROW + folded.shape[0], :] = folded

    def columns(x):
        t = x.T
        return jnp.concatenate(
            [jnp.broadcast_to(t[:, r : r + 1], (list_len, 128)) for r in range(regions)], axis=0
        )

    lane = lax.broadcasted_iota(jnp.int32, (1, 128), 1).astype(F32)
    ones = jnp.ones((128, 128), BF16)
    ids = columns(lists[...].astype(F32))
    line = jnp.floor(ids * (1.0 / 128.0))
    table_rows = placement.shape[0]
    line_hot = jnp.where(line == lane, 1.0, 0.0).astype(BF16)[:, :table_rows]
    at = lane == ids - 128.0 * line
    places = placement[...].astype(F32)
    high = jnp.floor(places * (1.0 / 64.0))

    def look(part):
        found = dot(line_hot, part.astype(BF16))
        return dot(jnp.where(at, found, 0.0).astype(BF16), ones)

    row = 64.0 * look(high) + look(places - 64.0 * high)
    holder = jnp.floor((row + 0.5) * (1.0 / blocks))
    inside = row - blocks * holder
    holder_band = jnp.floor((holder + 0.5) * (1.0 / lon_count))
    band_here = lax.axis_index("band")
    lon_here = lax.axis_index("lon")
    band_step = holder_band - band_here.astype(F32)
    lon_step = holder - lon_count * holder_band - lon_here.astype(F32)
    half = lon_count // 2
    lon_step = jnp.where(lon_step < -half, lon_step + lon_count, lon_step)
    lon_step = jnp.where(lon_step > half, lon_step - lon_count, lon_step)
    band_turn = band_step * (1 - 2 * (band_here % 2)).astype(F32)
    lon_turn = lon_step * (2 * (lon_here % 2) - 1).astype(F32)
    band_place = jnp.where(band_turn == 0.0, 0.0, jnp.where(band_turn > 0.0, 1.0, 2.0))
    lon_place = jnp.where(lon_turn == 0.0, 0.0, jnp.where(lon_turn > 0.0, 1.0, 2.0))
    key = (lon_place * 3.0 + band_place) * CLASS_STRIDE + inside

    hot = jnp.concatenate(
        [jnp.where(key == lane + 128.0 * c, 1.0, 0.0) for c in range(KEYS // 128)], axis=1
    ).astype(BF16)
    counts = lax.dot_general(
        hot,
        jnp.ones((entries, 128), BF16),
        (((0,), (0,)), ((), ())),
        preferred_element_type=F32,
    )
    present = jnp.minimum(counts, 1.0)
    down = lax.broadcasted_iota(jnp.int32, (KEYS, KEYS), 0)
    across = lax.broadcasted_iota(jnp.int32, (KEYS, KEYS), 1)
    before = (across < down) & (across // CLASS_STRIDE == down // CLASS_STRIDE)
    rank = dot(jnp.where(before, 1.0, 0.0).astype(BF16), present.astype(BF16))
    key_id = lax.broadcasted_iota(jnp.int32, (KEYS, 128), 0)
    slot = rank + (CAP * (key_id // CLASS_STRIDE)).astype(F32)
    block = (key_id % CLASS_STRIDE).astype(F32)
    slots = dot(hot, slot.astype(BF16))
    entry_slot[...] = slots
    tapers = columns(state[...])
    for c in range(2):
        match = (slot == lane + 128.0 * c) & (present > 0.0)
        rows = jnp.sum(jnp.where(match, block, 0.0), axis=0, keepdims=True)
        meta[BLOCK_ROW : BLOCK_ROW + 1, 128 * c : 128 * (c + 1)] = rows
        hit = jnp.where(slots == lane + 128.0 * c, tapers, 0.0)
        for r in range(regions):
            meta[r : r + 1, 128 * c : 128 * (c + 1)] = jnp.sum(
                hit[r * list_len : (r + 1) * list_len], axis=0, keepdims=True
            )
    transfers[-1].wait()


def weight_kernel(regions, list_len, entry_slot, taper, weights):
    obs_rows = taper.shape[1]
    group = (lax.broadcasted_iota(jnp.int32, (1, 128), 1) // obs_rows).astype(F32)
    p = lax.broadcasted_iota(jnp.int32, (obs_rows, 128), 0)
    q = lax.broadcasted_iota(jnp.int32, (obs_rows, 128), 1) % obs_rows
    spread = jnp.where(p == q, 1.0, 0.0).astype(BF16)

    def across(x):
        return lax.dot_general(
            x, spread, (((0,), (0,)), ((), ())), preferred_element_type=F32
        )

    for r in range(regions):
        mine = entry_slot[r * list_len : (r + 1) * list_len, :]
        high = taper[r].astype(BF16)
        low = (taper[r] - high.astype(F32)).astype(BF16)
        w = across(high) + across(low)
        for c in range(CLASSES * CAP // 4):
            hit = mine == group + 4.0 * c
            weights[r : r + 1, 128 * c : 128 * (c + 1)] = jnp.sum(
                jnp.where(hit, w, 0.0), axis=0, keepdims=True
            )


def gather_blocks(sources, table, first_slot, obs_rows, out):
    for k, source in enumerate(sources):
        for i in range(CAP):
            block = table[BLOCK_ROW, first_slot + CAP * k + i].astype(jnp.int32)
            at = pl.multiple_of(block * obs_rows, obs_rows)
            to = (CAP * k + i) * obs_rows
            out[to : to + obs_rows, :] = source[pl.ds(at, obs_rows), :]


def select_kernel(obs_rows, obs, obs_1, obs_2, table_1, table_2, to_1, to_2):
    sources = (obs, obs_1, obs_2)
    gather_blocks(sources, table_1, FIRST * BAND_SLOTS, obs_rows, to_1)
    gather_blocks(sources, table_2, SECOND * BAND_SLOTS, obs_rows, to_2)


def transposed(y):
    return jnp.concatenate(
        [y[256 * c : 256 * (c + 1)].astype(F32).T.astype(BF16) for c in range(y.shape[0] // 256)],
        axis=1,
    )


def near_gram_kernel(obs_rows, regions, obs, obs_1, obs_2, pool_2, table, weights, gram, pool):
    gather_blocks((obs, obs_1, obs_2), table, SELF * BAND_SLOTS, obs_rows, pool)
    size = pool.shape[0]
    parts = [(y[...], transposed(y[...]), at * size) for y, at in ((pool, SELF), (pool_2, SECOND))]
    for r in range(regions):
        gram[256 * r : 256 * (r + 1), :] = gram_of(r, weights, parts)


def gram_of(r, weights, parts):
    products = [
        dot(y_t * weights[r : r + 1, lane : lane + y.shape[0]].astype(BF16), y)
        for y, y_t, lane in parts
    ]
    return sum(products[1:], products[0])


def innov_kernel(obs_rows, regions, blocks, metas, metas_1, metas_2, weights, pool, pool_2, scaled, proj):
    down = lax.broadcasted_iota(jnp.int32, (blocks, META_LANES), 0).astype(F32)
    mine = metas[META_ROWS * SELF + BLOCK_ROW : META_ROWS * SELF + BLOCK_ROW + 1, :]
    hot = jnp.where(down == mine, 1.0, 0.0).T.astype(BF16)
    per = META_LANES // obs_rows
    sub = lax.broadcasted_iota(jnp.int32, (per, META_LANES), 0)
    which = lax.broadcasted_iota(jnp.int32, (per, META_LANES), 1) // obs_rows
    picked = []
    for n in range(CLASSES):
        source = (metas, metas_1, metas_2)[n % 3]
        base = META_ROWS * (n // 3) + INNOV_ROW
        rows = [
            jnp.where(sub == which, source[base + i : base + i + 1, :], 0.0)
            for i in range(blocks // per)
        ]
        picked.append(dot(hot[CAP * n : CAP * (n + 1)], jnp.concatenate(rows, axis=0).astype(BF16)))
    p = lax.broadcasted_iota(jnp.int32, (META_LANES, META_LANES), 0) % obs_rows
    q = lax.broadcasted_iota(jnp.int32, (META_LANES, META_LANES), 1) % obs_rows
    spread = jnp.where(p == q, 1.0, 0.0).astype(BF16)
    repeated = dot(jnp.concatenate(picked, axis=0).astype(BF16), spread)
    folded = fold(repeated, obs_rows)
    lanes = jnp.concatenate([folded[i : i + 1] for i in range(folded.shape[0])], axis=1)
    wd = weights[...] * lanes
    high = wd.astype(BF16)
    both = jnp.concatenate([high.astype(F32), wd - high.astype(F32)], axis=0).astype(BF16)
    scaled[...] = both
    size = pool.shape[0]
    part = dot(both[:, SELF * size : (SELF + 1) * size], pool[...])
    part = part + dot(both[:, SECOND * size : (SECOND + 1) * size], pool_2[...])
    proj[...] = part[:regions] + part[regions:]


def quarters(x):
    return x[:128, :128], x[:128, 128:], x[128:, :128], x[128:, 128:]


def add_diagonal(x, d, eye):
    q = quarters(x)
    top = jnp.concatenate([q[0] + d * eye, q[1]], axis=1)
    low = jnp.concatenate([q[2], q[3] + d * eye], axis=1)
    return jnp.concatenate([top, low], axis=0)


def trace(x, eye):
    q = quarters(x)
    both = (q[0] + q[3]) * eye
    return jnp.sum(jnp.sum(both, axis=0, keepdims=True), axis=1, keepdims=True)


def roots(grams, proj_rows, eye, ensemble, between):
    each = range(len(grams))
    base = ensemble - 1.0
    scale = [
        base
        + jnp.max(jnp.sum(jnp.abs(grams[i]), axis=0, keepdims=True), axis=1, keepdims=True)
        for i in each
    ]
    inverse = [1.0 / scale[i] for i in each]
    mean = [trace(grams[i], eye) * (1.0 / ensemble) for i in each]
    u = [
        add_diagonal(grams[i] * (-0.5 * inverse[i]), 0.5 * inverse[i] * mean[i], eye)
        for i in each
    ]
    c = [1.0 - (base + mean[i]) * inverse[i] for i in each]
    a = [1.0 + 0.5 * c[i] for i in each]
    g = u
    ub = [u[i].astype(BF16) for i in each]
    gb = ub
    for step in range(NS_ITERS - 1):
        u2 = [dot(ub[i], ub[i]) for i in each]
        w = [((1.5 + 1.5 * c[i]) * u[i] + u2[i]).astype(BF16) for i in each]
        u3 = [dot(ub[i], w[i]) for i in each]
        between()
        u = [(1.5 * c[i] + 0.75 * c[i] * c[i]) * u[i] + u3[i] for i in each]
        c = [(0.75 + 0.25 * c[i]) * c[i] * c[i] for i in each]
        ub = [u[i].astype(BF16) for i in each]
        ug = [dot(ub[i], gb[i]) for i in each]
        g = [(1.0 + 0.5 * c[i]) * g[i] + a[i] * u[i] + ug[i] for i in each]
        gb = [g[i].astype(BF16) for i in each]
        a = [a[i] * (1.0 + 0.5 * c[i]) for i in each]
    first = lax.broadcasted_iota(jnp.int32, (16, ensemble), 0) < 8

    def times(i, v):
        high = v.astype(BF16).astype(F32)
        stacked = jnp.where(first, high, v - high).astype(BF16)
        q = dot(stacked, gb[i])
        return a[i] * v + q[0:1] + q[8:9]

    half = [times(i, proj_rows[i]) for i in each]
    wbar = [times(i, half[i]) * inverse[i] for i in each]
    factor = [lax.sqrt(base * inverse[i]) for i in each]
    return [(factor[i], factor[i] * a[i] - 1.0, g[i]) for i in each], wbar


EXTRAS = 5


def packed_rows(regions):
    return regions * 256 + -(-EXTRAS * regions // 16) * 16


def pack(matrix, wbar, eye, upper):
    factor, diagonal, g = matrix
    q = quarters(g)
    left = factor * q[0] + diagonal * eye
    right = factor * q[1]
    corner = factor * q[3] + diagonal * eye
    merged = jnp.where(upper, left, corner)
    high = wbar.astype(BF16).astype(F32)
    low = wbar - high
    extra = [
        jnp.sum(corner * eye, axis=0, keepdims=True),
        high[:, :128],
        high[:, 128:],
        low[:, :128],
        low[:, 128:],
    ]
    return right.astype(BF16), merged.astype(BF16), extra


def mix_regions(first, count, gram, proj, packed, between):
    n = 256
    down = lax.broadcasted_iota(jnp.int32, (128, 128), 0)
    across = lax.broadcasted_iota(jnp.int32, (128, 128), 1)
    eye = jnp.where(down == across, 1.0, 0.0)
    some = range(first, first + count)
    matrices, weights = roots(
        [gram[r - first] for r in some], [proj[r : r + 1, :] for r in some], eye, n, between
    )
    extras = []
    for k, r in enumerate(some):
        right, merged, extra = pack(matrices[k], weights[k], eye, down <= across)
        packed[n * r : n * r + 128, :] = right
        packed[n * r + 128 : n * (r + 1), :] = merged
        extras.append(extra)
    return extras


def mix_kernel(together, pool, weights, gram_near, scaled, proj_near, packed, proj):
    regions = proj.shape[0]
    size = pool.shape[0]
    part = dot(scaled[:, FIRST * size : (FIRST + 1) * size], pool[...])
    proj[...] = proj_near[...] + part[:regions] + part[regions:]
    parts = [(pool[...], transposed(pool[...]), FIRST * size)]

    def gram(r):
        return gram_near[256 * r : 256 * (r + 1), :] + gram_of(r, weights, parts)

    extras = []
    ready = [gram(r) for r in range(together)]
    for first in range(0, regions, together):
        later = []
        rest = list(range(first + together, min(first + 2 * together, regions)))

        def between(rest=rest, later=later):
            if rest:
                later.append(gram(rest.pop(0)))

        extras += mix_regions(first, together, ready, proj, packed, between)
        ready = later + [gram(r) for r in rest]
    rows = packed.shape[0] - 256 * regions
    below = jnp.zeros((rows - EXTRAS * regions, 128), F32)
    stacked = [extras[r][k] for k in range(EXTRAS) for r in range(regions)] + [below]
    packed[256 * regions :, :] = jnp.concatenate(stacked, axis=0).astype(BF16)


def unpack(count, packed, full):
    n = 256
    down = lax.broadcasted_iota(jnp.int32, (128, 128), 0)
    across = lax.broadcasted_iota(jnp.int32, (128, 128), 1)
    upper = down <= across
    lower = down > across
    extra = packed[n * count :, :].astype(F32)
    below = jnp.zeros((128 - extra.shape[0], 128), F32)
    columns = jnp.concatenate([extra, below], axis=0).T.astype(BF16)

    def spread(k):
        both = (down == k) | (down == k + 2 * count)
        return dot(columns, jnp.where(both, 1.0, 0.0).astype(BF16))

    for k in range(count):
        right = packed[n * k : n * k + 128, :].astype(F32)
        merged = packed[n * k + 128 : n * (k + 1), :].astype(F32)
        turned = merged.T
        top = spread(count + k)
        low = spread(2 * count + k)
        diagonal = extra[k : k + 1]
        corner = jnp.where(lower, merged, jnp.where(down == across, diagonal, turned))
        full[n * k : n * k + 128, :128] = (jnp.where(upper, merged, turned) + top).astype(BF16)
        full[n * k : n * k + 128, 128:] = (right + top).astype(BF16)
        full[n * k + 128 : n * (k + 1), :128] = (right.T + low).astype(BF16)
        full[n * k + 128 : n * (k + 1), 128:] = (corner + low).astype(BF16)


def block_places(table, first_slot, state_rows):
    return [
        pl.multiple_of(table[BLOCK_ROW, first_slot + i].astype(jnp.int32) * state_rows, state_rows)
        for i in range(CAP)
    ]


def scale_members(members, table, first_slot, places, count, left, state_rows):
    n = members.shape[1]
    for i in range(CAP):
        x = members[pl.ds(places[i], state_rows), :]
        for k in range(count):
            t = jnp.full((16, 128), table[k, first_slot + i], F32).astype(BF16)
            for u in range(state_rows // 16):
                for v in range(n // 128):
                    left[
                        state_rows * i + 16 * u : state_rows * i + 16 * (u + 1),
                        n * k + 128 * v : n * k + 128 * (v + 1),
                    ] = x[16 * u : 16 * (u + 1), 128 * v : 128 * (v + 1)] * t


def add_products(left, full, places, acc, state_rows):
    product = dot(left[...], full[...])
    for i in range(CAP):
        acc[pl.ds(places[i], state_rows), :] += product[state_rows * i : state_rows * (i + 1), :]


def increment_kernel(slots, halves, next_slots, start, state_rows, count, *refs):
    refs = list(refs)
    members = refs.pop(0)
    before = None if start else refs.pop(0)
    items, ahead = len(slots), len(next_slots)
    tables, refs = refs[: items + ahead], refs[items + ahead :]
    packed, refs = refs[:items], refs[items:]
    acc, lefts, scratch = refs[0], refs[1 : 1 + ahead], refs[1 + ahead :]
    rows = packed_rows(count)
    acc[...] = members[...].astype(F32) if start else before[...]
    for k, slot in enumerate(slots):
        left, full = scratch[2 * (k % 2) : 2 * (k % 2) + 2]
        places = block_places(tables[k], slot, state_rows)
        unpack(count, packed[k].at[rows * halves[k] : rows * (halves[k] + 1), :], full)
        scale_members(members, tables[k], slot, places, count, left, state_rows)
        add_products(left, full, places, acc, state_rows)
    for k, slot in enumerate(next_slots):
        table = tables[items + k]
        places = block_places(table, slot, state_rows)
        scale_members(members, table, slot, places, count, lefts[k], state_rows)


def finish_kernel(slots, halves, state_rows, count, before, *refs):
    items = len(slots)
    tables, packed, lefts = refs[:items], refs[items : 2 * items], refs[2 * items : 3 * items]
    out, acc, *fulls = refs[3 * items :]
    rows = packed_rows(count)
    acc[...] = before[...]
    for k in range(items):
        unpack(count, packed[k].at[rows * halves[k] : rows * (halves[k] + 1), :], fulls[k])
        places = block_places(tables[k], slots[k], state_rows)
        add_products(lefts[k], fulls[k], places, acc, state_rows)
    out[...] = acc[...].astype(BF16)


def from_band(x, place):
    count = lax.axis_size("band")
    step = 1 if place == FIRST else -1
    pairs = [(i + step * (1 - 2 * (i % 2)), i) for i in range(count)]
    return lax.ppermute(x, "band", [(j, i) for j, i in pairs if 0 <= j < count])


def from_lon(x, place):
    count = lax.axis_size("lon")
    step = -1 if place == FIRST else 1
    return lax.ppermute(
        x, "lon", [((i + step * (1 - 2 * (i % 2))) % count, i) for i in range(count)]
    )


def local(members, obs_perts, innovations, lists, placement, obs_taper, state_taper):
    lon_count = lax.axis_size("lon")
    blocks, state_rows, n = members.shape
    obs_rows = obs_perts.shape[1]
    regions, list_len = lists.shape
    entries = regions * list_len

    obs = obs_perts.reshape(blocks * obs_rows, n)
    obs_1 = from_band(obs, FIRST)
    obs_2 = from_band(obs, SECOND)

    meta, entry_slot, obs = call(
        functools.partial(table_kernel, (lon_count, blocks)),
        (
            jax.ShapeDtypeStruct((META_ROWS, META_LANES), F32),
            jax.ShapeDtypeStruct((entries, 128), F32),
            jax.ShapeDtypeStruct(obs.shape, BF16),
        ),
        [HBM_SPEC] * 5,
        "tables",
        10**9,
        10**6,
        [
            pltpu.VMEM(lists.shape, jnp.int32),
            pltpu.VMEM((placement.shape[0] // 128, 128), jnp.int32),
            pltpu.VMEM(state_taper.shape, F32),
            pltpu.VMEM(innovations.shape, BF16),
            pltpu.SemaphoreType.DMA((5,)),
        ],
    )(lists, placement.reshape(-1, 128), state_taper, innovations, obs)
    meta_1 = from_lon(meta, FIRST)
    meta_2 = from_lon(meta, SECOND)

    weights = call(
        functools.partial(weight_kernel, regions, list_len),
        jax.ShapeDtypeStruct((regions, CLASSES * CAP * obs_rows), F32),
        [VMEM_SPEC] * 2,
        "weights",
        10**9,
        10**6,
    )(entry_slot, jnp.swapaxes(obs_taper, 1, 2))
    obs_2, obs_1, weights = lax.optimization_barrier((obs_2, obs_1, weights))
    size = BAND_SLOTS * obs_rows
    pool_shape = jax.ShapeDtypeStruct((size, n), BF16)
    to_1, to_2 = call(
        functools.partial(select_kernel, obs_rows),
        (pool_shape, pool_shape),
        [VMEM_SPEC] * 3 + [SMEM_SPEC] * 2,
        "select",
        10**8,
        4 * 10**6,
    )(obs, obs_1, obs_2, meta_1, meta_2)
    pool_1 = from_lon(to_1, FIRST)
    pool_2 = from_lon(to_2, SECOND)
    metas = jnp.concatenate([meta, meta_1, meta_2], axis=0)
    metas_1 = from_band(metas, FIRST)
    metas_2 = from_band(metas, SECOND)

    region_flops = 2 * n**3
    gram_near, pool = call(
        functools.partial(near_gram_kernel, obs_rows, regions),
        (jax.ShapeDtypeStruct((regions * n, n), F32), pool_shape),
        [VMEM_SPEC] * 4 + [SMEM_SPEC] + [VMEM_SPEC],
        "near_gram",
        regions * 12 * region_flops,
        5 * 10**6,
    )(obs, obs_1, obs_2, pool_2, meta, weights)
    metas_2, metas_1, pool = lax.optimization_barrier((metas_2, metas_1, pool))
    proj_shape = jax.ShapeDtypeStruct((regions, n), F32)
    scaled, proj_near = call(
        functools.partial(innov_kernel, obs_rows, regions, blocks),
        (jax.ShapeDtypeStruct((2 * regions, 3 * size), BF16), proj_shape),
        [VMEM_SPEC] * 6,
        "innov",
        10**8,
        2 * 10**6,
    )(metas, metas_1, metas_2, weights, pool, pool_2)
    mix = call(
        functools.partial(mix_kernel, 4),
        jax.ShapeDtypeStruct((packed_rows(regions), 128), BF16),
        [VMEM_SPEC] * 5,
        "mixing",
        regions * 18 * region_flops,
        4 * 10**6,
        [pltpu.VMEM(proj_shape.shape, F32)],
    )(pool_1, weights, gram_near, scaled, proj_near)

    stacked = (metas, metas_1, metas_2)

    def table(lon, band):
        return stacked[band][META_ROWS * lon : META_ROWS * (lon + 1)]

    def slots(lon, band):
        return CAP * (lon * 3 + band)

    flat = members.reshape(blocks * state_rows, n)
    acc_shape = jax.ShapeDtypeStruct((blocks * state_rows, n), F32)
    scratch = [
        pltpu.VMEM((CAP * state_rows, regions * n), BF16),
        pltpu.VMEM((regions * n, n), BF16),
    ] * 2

    left_shape = jax.ShapeDtypeStruct((CAP * state_rows, regions * n), BF16)

    def increments(acc, groups, ahead, name):
        start = acc is None
        kernel = functools.partial(
            increment_kernel,
            [slots(*g) for g in groups],
            [arrived[g][1] for g in groups],
            [slots(*g) for g in ahead],
            start,
            state_rows,
            regions,
        )
        return call(
            kernel,
            (acc_shape,) + (left_shape,) * len(ahead),
            [VMEM_SPEC] * (1 if start else 2)
            + [SMEM_SPEC] * (len(groups) + len(ahead))
            + [VMEM_SPEC] * len(groups),
            name,
            len(groups) * 3 * regions * region_flops,
            6 * 10**6,
            scratch,
        )(
            *([flat] if start else [flat, acc]),
            *[table(*g) for g in groups + ahead],
            *[arrived[g][0] for g in groups],
        )

    arrived = {(SELF, SELF): (mix, 0)}
    for lon in (SECOND, FIRST):
        arrived[lon, SELF] = (from_lon(mix, lon), 0)
    mix_2 = from_band(mix, SECOND)
    mix_1 = from_band(mix, FIRST)
    last = [(FIRST, FIRST), (FIRST, SECOND)]
    acc, *lefts = increments(None, [(SELF, SELF), (SECOND, SELF)], last, "own")
    mix_1, mix_2, near, acc = lax.optimization_barrier(
        (mix_1, mix_2, arrived[FIRST, SELF][0], acc)
    )
    arrived[FIRST, SELF] = (near, 0)
    arrived[FIRST, FIRST] = (from_band(near, FIRST), 0)
    arrived[FIRST, SECOND] = (from_band(near, SECOND), 0)
    arrived[SELF, FIRST], arrived[SELF, SECOND] = (mix_1, 0), (mix_2, 0)
    both = from_lon(jnp.concatenate([mix_1, mix_2], axis=0), SECOND)
    arrived[SECOND, FIRST], arrived[SECOND, SECOND] = (both, 0), (both, 1)
    (acc,) = increments(acc, [(SELF, FIRST), (SELF, SECOND), (FIRST, SELF)], [], "inner")
    (acc,) = increments(acc, [(SECOND, FIRST), (SECOND, SECOND)], [], "outer")
    out = call(
        functools.partial(
            finish_kernel,
            [slots(*g) for g in last],
            [arrived[g][1] for g in last],
            state_rows,
            regions,
        ),
        jax.ShapeDtypeStruct(acc_shape.shape, BF16),
        [VMEM_SPEC] + [SMEM_SPEC] * 2 + [VMEM_SPEC] * 4,
        "finish",
        6 * regions * region_flops,
        9 * 10**6,
        [pltpu.VMEM(acc_shape.shape, F32)] + [pltpu.VMEM((regions * n, n), BF16)] * 2,
    )(acc, *[table(*g) for g in last], *[arrived[g][0] for g in last], *lefts)
    return out.reshape(members.shape)


def solution(mesh):
    in_specs = (
        P(("band", "lon"), None, None),
        P(("band", "lon"), None, None),
        P(("band", "lon"), None),
        P(("band", "lon"), None),
        P(),
        P(("band", "lon"), None, None),
        P(("band", "lon"), None),
    )
    out_specs = P(("band", "lon"), None, None)
    return jax.shard_map(local, mesh=mesh, in_specs=in_specs, out_specs=out_specs, check_vma=False)
```
